32 devices in a mesh: group: 2 (over y), expert: 4 (over z), req: 4 (over x, core).
Axes of the slice: x: 2, y: 2, z: 4, core: 2. Of those that a mesh axis runs over, the one named last changes fastest.
Arguments:
- verify_in: bfloat16 [128, 4096], P(('group', 'expert'), 'req'), parts along dimension 0, may hold values from -6 to 6
- expert_ids: int32 [128, 2], P(('group', 'expert')), parts along dimension 0, may hold values from 0 to 7, all different within a row; in each aligned block of 16 rows (0 to 15, 16 to 31, ...) at most 8 rows name the same one
- gate_weights: float32 [128, 2], P(('group', 'expert')), parts along dimension 0, may hold values from 0.2 to 1
- moe_gate: bfloat16 [32, 4096, 1792], P('expert', None, 'req'), may hold values from -0.09375 to 0.09375
- moe_up: bfloat16 [32, 4096, 1792], P('expert', None, 'req'), may hold values from -0.09375 to 0.09375
- moe_down: bfloat16 [32, 1792, 4096], P('expert', 'req'), may hold values from -0.09375 to 0.09375
- draft_emb: bfloat16 [2048, 4096], P(('group', 'req'), 'expert'), parts along dimension 0, may hold values from -6 to 6
- draft_feat: bfloat16 [2048, 4096], P(('group', 'req'), 'expert'), parts along dimension 0, may hold values from -18 to 18
- parents: int32 [2048], P(('group', 'req')), parts along dimension 0, may hold values from 0 to 1023, as said below
- join_weight: bfloat16 [8192, 4096], P('req', 'expert'), may hold values from -3 to 3
- norm_gain: float32 [4096], P('expert'), may hold values from 0.5 to 1.5
- draft_gate: bfloat16 [4096, 7168], P('req', 'expert'), may hold values from -0.09375 to 0.09375
- draft_up: bfloat16 [4096, 7168], P('req', 'expert'), may hold values from -0.09375 to 0.09375
- draft_down: bfloat16 [7168, 4096], P('expert', 'req'), may hold values from -0.09375 to 0.09375
Outputs:
- verify_out: bfloat16 [128, 4096], P(('group', 'expert'), 'req'), parts along dimension 0
- draft_out: bfloat16 [2048, 4096], P(('group', 'req'), 'expert'), parts along dimension 0
The draws below stay inside these ranges and needn't reach their ends.
There are 2 independent parts, one for each index of `group`. The reference program is written for one: setup_inputs(seed, part) draws one part's arguments, and reference() takes and returns one part's arrays. A program takes and returns all parts, laid end to end along the dimension named above; an argument that names none is the same for every part. Nothing has to cross between parts.
Inputs may be any that keep to these rules, and one draw needn't show every extreme that they name: `expert_ids`: each row names two different experts; within the rows of one index of expert, no expert is named more than 8 times. `parents`: each row's parent is a row of the same tree of 64 consecutive rows at an earlier position; a tree's first row is its own parent.
All inputs are finite; a program needn't handle non-finite values.
Results may differ from the reference program's by a relative error of at most 0.015.
Values may be sent and summed in bfloat16 or wider, within the bound.
A program may use at most 256 MiB of HBM per device.

```python
import math
import jax
import jax.numpy as jnp
import numpy as np
from jax import lax

D = 4096
EXPERTS = 8
FF = 7168
DFF = 7168
SLICES = 4
TREE = 64
VROW_DEV = 16
CAP = 8
VROWS = 64
DROWS = 1024
N_EXPERT = 4
N_REQ = 4


def draw_draft_feat(key, part):
    base_key, scale_key = jax.random.split(jax.random.fold_in(key, 11), 2)
    base = jnp.clip(jax.random.normal(base_key, (DROWS, D), jnp.float32), -6.0, 6.0)
    scales = jnp.exp(jax.random.uniform(scale_key, (DROWS, 1), jnp.float32, math.log(0.3), math.log(3.0)))
    return (base * scales).astype(jnp.bfloat16)


def draw_join_weight(key, part):
    base_key, jitter_key = jax.random.split(jax.random.fold_in(key, 23), 2)
    positions = jnp.arange(D, dtype=jnp.float32) / D
    rising = jnp.exp(math.log(3.0) * (positions - 0.5))[None, :]
    jitter = jnp.exp(jax.random.uniform(jitter_key, (1, D), jnp.float32, -1.15, 1.15))
    column_scale = rising * jitter / math.sqrt(2.0 * D)
    base = jnp.clip(jax.random.normal(base_key, (2 * D, D), jnp.float32), -6.0, 6.0)
    return (base * column_scale).astype(jnp.bfloat16)


def draw_parents(key, part):
    position = jnp.arange(DROWS, dtype=jnp.int32)
    within = position % TREE
    offsets = jax.random.randint(jax.random.fold_in(key, 7), (DROWS,), 0, jnp.maximum(within, 1), jnp.int32)
    return (position - within + offsets).astype(jnp.int32)


def raised(array, stream_key, source, target, shards_of, factor):
    def block_of(dim):
        return (jnp.arange(array.shape[dim]) // (array.shape[dim] // shards_of)).reshape((-1,) + (1,) * (array.ndim - 1 - dim))

    first = jax.random.permutation(stream_key, shards_of)[block_of(target)]
    other_side = (block_of(target) + shards_of // 2) % shards_of
    return jnp.where((block_of(source) == first) | (block_of(source) == other_side), factor * array, array)


def level_of(rng, extent, shards, smallest, largest):
    gain, own = 1.0, jax.random.fold_in(rng, 6)
    for dim, blocks in shards:
        draws = jnp.exp(jax.random.uniform(jax.random.fold_in(own, dim), (blocks,), jnp.float32, smallest / len(shards), largest / len(shards)))
        gain = gain * jnp.repeat(draws, extent[dim] // blocks).reshape([-1 if axis == dim else 1 for axis in range(len(extent))])
    return gain


def deal_out(stream_key, own, number, rows, amount, top, bound, lean):
    sequence = jax.random.permutation(stream_key, amount)
    heavy_load, ordinary = portions_of(amount, rows * top, bound, lean, True), portions_of(amount, rows * top, bound, lean, False)
    places = jnp.arange(amount)

    def named(sizes, offset_by):
        used = int((sizes > 0).sum())
        fixed = max(1, used // 4)
        moved = fixed + (places - fixed + offset_by * (used - fixed)) % max(1, amount - fixed)
        return jnp.zeros((amount,), jnp.int32).at[sequence[jnp.where(places < fixed, places, moved)]].set(jnp.asarray(sizes, jnp.int32))

    sizes = jnp.where(number % 4 == 0, named(heavy_load, number // 4), named(ordinary, number - number // 4 - 1))
    mixed = jax.random.permutation(jax.random.fold_in(own, 3), amount)
    giver, receiver = mixed[0:amount // 2 * 2:2], mixed[1:amount // 2 * 2:2]
    slack = jnp.minimum(sizes[giver] - 1, bound - sizes[receiver]) // 2
    slack = jnp.where((giver == sequence[0]) | (receiver == sequence[0]) | (sizes[receiver] == 0), 0, jnp.maximum(slack, 0))
    moved = jax.random.randint(jax.random.fold_in(own, 4), (amount // 2,), 0, 1 << 20) % (slack + 1)
    sizes = sizes.at[giver].add(-moved).at[receiver].add(moved)
    items = jnp.searchsorted(jnp.cumsum(sizes), jnp.arange(rows * top), side="right").astype(jnp.int32)
    grid = items.reshape(top, rows).T
    grid = grid[jax.random.permutation(jax.random.fold_in(own, 1), rows)]
    offset_by = jax.random.randint(jax.random.fold_in(own, 2), (rows, 1), 0, top)
    return jnp.take_along_axis(grid, (jnp.arange(top)[None, :] + offset_by) % top, axis=1)


def portions_of(count, total, bound, skew, full):
    weights = [(1 << 20) // math.isqrt(grade ** skew) + 1 for grade in range(1, count + 1)]
    largest = bound if full else min(bound, max(-(-total // count), total * weights[0] // sum(weights)))
    least = 1 if total - largest >= count - 1 else 0
    given, spare = [largest] + [least] * (count - 1), total - largest - least * (count - 1)
    while spare > 0:
        free = [i for i in range(1, count) if given[i] < largest] or [i for i in range(1, count) if given[i] < bound]
        pool, left = sum([weights[i] for i in free]), spare
        for i in free:
            extra = min(bound - given[i], max(1, left * weights[i] // pool), spare)
            given[i] = given[i] + extra
            spare = spare - extra
    return np.array(given)


def noise(rng, dims, width, bound, cuts=(), kind=jnp.bfloat16):
    factor_of = level_of(rng, dims, cuts, -0.22, 0.18) if cuts else 1.0
    drawn = jax.random.normal(rng, dims, jnp.float32) * width * factor_of
    return jnp.minimum(jnp.maximum(drawn, -bound), bound).astype(kind)


def heavy_noise(key, extent, spread, most, cuts, heavy, held_as=jnp.bfloat16):
    entries = spread * jax.random.normal(key, extent, jnp.float32)
    if cuts:
        entries = entries * level_of(key, extent, cuts, -0.22, 0.18)
    return jnp.clip(raised(entries, jax.random.fold_in(key, 3), *heavy), -most, most).astype(held_as)


def setup_inputs(seed: int = 0, part: int = 0) -> dict:
    seeds = jax.random.split(jax.random.key(seed), 15)
    part_keys = jax.random.split(jax.random.fold_in(seeds[14], part), 15)
    verify_in = noise(part_keys[0], (VROWS, D), 1.0, 6.0, ((0, 4), (1, 4)))
    expert_ids_keys = jax.random.split(jax.random.fold_in(part_keys[1], 1), VROWS // VROW_DEV)
    expert_ids_turns = jax.random.permutation(jax.random.fold_in(part_keys[1], 3), VROWS // VROW_DEV)
    expert_ids = jax.vmap(lambda own, number: deal_out(jax.random.fold_in(part_keys[1], 2), own, number, VROW_DEV, EXPERTS, 2, CAP, 2))(expert_ids_keys, expert_ids_turns).reshape((VROWS, 2))
    gate_weights = jnp.clip(0.2 + 0.8 * jax.random.uniform(part_keys[2], (VROWS, 2), jnp.float32) ** level_of(part_keys[2], (VROWS, 2), ((0, 4),), -0.2, 0.2), 0.2, 1.0)
    moe_gate = noise(seeds[3], (EXPERTS * SLICES, D, FF // SLICES), D ** -0.5, 0.09375, ((0, 4), (2, 4)))
    moe_up = noise(seeds[4], (EXPERTS * SLICES, D, FF // SLICES), D ** -0.5, 0.09375, ((0, 4), (2, 4)))
    moe_down = heavy_noise(seeds[5], (EXPERTS * SLICES, FF // SLICES, D), FF ** -0.5, 0.09375, ((0, 4), (1, 4)), (1, 2, 4, 2.0))
    draft_emb = noise(part_keys[6], (DROWS, D), 1.0, 6.0, ((0, 4), (1, 4)))
    draft_feat = draw_draft_feat(jax.random.fold_in(jax.random.fold_in(seeds[14], part), 71), part)
    parents = draw_parents(jax.random.fold_in(jax.random.fold_in(seeds[14], part), 71), part)
    join_weight = draw_join_weight(jax.random.fold_in(seeds[14], 71), part)
    norm_gain = jnp.clip(1.0 + 0.1 * jax.random.normal(seeds[10], (D,), jnp.float32), 0.5, 1.5)
    draft_gate = noise(seeds[11], (D, DFF), D ** -0.5, 0.09375, ((0, 4), (1, 4)))
    draft_up = noise(seeds[12], (D, DFF), D ** -0.5, 0.09375, ((0, 4), (1, 4)))
    draft_down = heavy_noise(seeds[13], (DFF, D), DFF ** -0.5, 0.09375, ((0, 4), (1, 4)), (0, 1, 4, 2.0))
    return dict(verify_in=verify_in, expert_ids=expert_ids, gate_weights=gate_weights, moe_gate=moe_gate, moe_up=moe_up, moe_down=moe_down, draft_emb=draft_emb, draft_feat=draft_feat, parents=parents, join_weight=join_weight, norm_gain=norm_gain, draft_gate=draft_gate, draft_up=draft_up, draft_down=draft_down)


def slot_numbers(expert_ids):
    blocks = expert_ids.reshape(N_EXPERT, VROW_DEV * 2)
    onehot = (blocks[:, :, None] == jnp.arange(EXPERTS, dtype=jnp.int32)[None, None, :]).astype(jnp.int32)
    before = jnp.cumsum(onehot, axis=1) - onehot
    return lax.optimization_barrier(jnp.sum(before * onehot, axis=2)).reshape(VROWS, 2).astype(jnp.int32)

def verify_layer(verify_in, expert_ids, gate_weights, moe_gate, moe_up, moe_down):
    slot_index = slot_numbers(expert_ids)
    row_ids = jnp.arange(VROWS, dtype=jnp.int32)
    position = ((row_ids // VROW_DEV)[:, None] * CAP + slot_index).astype(jnp.int32)
    table = jnp.full((EXPERTS, N_EXPERT * CAP), VROWS, jnp.int32)
    table = table.at[expert_ids, position].set(jnp.broadcast_to(row_ids[:, None], (VROWS, 2)).astype(jnp.int32))
    padded = jnp.concatenate([verify_in, jnp.zeros((1, D), jnp.bfloat16)], axis=0)
    slice_width = FF // SLICES
    pieces = SLICES * N_REQ
    piece_width = FF // pieces

    def one_expert(inputs):
        chosen_rows, gate_w, up_w, down_w = inputs
        chosen = padded[chosen_rows]
        gate_full = jnp.transpose(gate_w, (1, 0, 2)).reshape(D, FF)
        up_full = jnp.transpose(up_w, (1, 0, 2)).reshape(D, FF)
        gate_sum = jnp.dot(chosen, gate_full, preferred_element_type=jnp.float32)
        up_sum = jnp.dot(chosen, up_full, preferred_element_type=jnp.float32)
        hidden = (jax.nn.silu(gate_sum) * up_sum).astype(jnp.bfloat16)
        hidden_parts = hidden.reshape(hidden.shape[0], pieces, piece_width).astype(jnp.float32)
        down_parts = down_w.reshape(pieces, piece_width, D).astype(jnp.float32)
        partial_value = jnp.einsum('mpq,pqd->pmd', hidden_parts, down_parts)
        rounded = lax.optimization_barrier(partial_value.astype(jnp.bfloat16))
        result = lax.optimization_barrier(jnp.sum(rounded.astype(jnp.float32), axis=0))
        return result.astype(jnp.bfloat16)
    outputs = lax.map(one_expert, (table, moe_gate.reshape(EXPERTS, SLICES, D, slice_width), moe_up.reshape(EXPERTS, SLICES, D, slice_width), moe_down.reshape(EXPERTS, SLICES, slice_width, D)))
    picked = outputs[expert_ids, position].astype(jnp.float32)
    return lax.optimization_barrier(jnp.sum(gate_weights[:, :, None] * picked, axis=1)).astype(jnp.bfloat16)

def draft_step(draft_emb, draft_feat, parents, join_weight, norm_gain, draft_gate, draft_up, draft_down):
    joined = jnp.concatenate([draft_emb, draft_feat[parents]], axis=1)
    joined_state = jnp.dot(joined, join_weight, preferred_element_type=jnp.float32)
    meansq = lax.optimization_barrier(jnp.mean(joined_state * joined_state, axis=1, keepdims=True))
    normed = (joined_state * lax.rsqrt(meansq + 1e-05) * norm_gain[None, :]).astype(jnp.bfloat16)
    gate_sum = jnp.dot(normed, draft_gate, preferred_element_type=jnp.float32)
    up_sum = jnp.dot(normed, draft_up, preferred_element_type=jnp.float32)
    hidden = (jax.nn.silu(gate_sum) * up_sum).astype(jnp.bfloat16)
    mlp_sum = jnp.dot(hidden, draft_down, preferred_element_type=jnp.float32)
    return (joined_state + mlp_sum).astype(jnp.bfloat16)

def reference(verify_in, expert_ids, gate_weights, moe_gate, moe_up, moe_down, draft_emb, draft_feat, parents, join_weight, norm_gain, draft_gate, draft_up, draft_down):
    verify_out = verify_layer(verify_in, expert_ids, gate_weights, moe_gate, moe_up, moe_down)
    draft_out = draft_step(draft_emb, draft_feat, parents, join_weight, norm_gain, draft_gate, draft_up, draft_down)
    return (verify_out, draft_out)
```

```python
import jax
import jax.numpy as jnp
from jax import lax
from jax.sharding import PartitionSpec as P

EXPERTS = 8
EPS = 1e-05


def verify_layer(verify_in, expert_ids, gate_weights, moe_gate, moe_up, moe_down):
    n_expert, n_req = lax.axis_size("expert"), lax.axis_size("req")
    own_rows, own_width = verify_in.shape
    local = moe_gate.shape[0]
    slices = local * n_expert // EXPERTS
    rows, width = own_rows * n_expert, own_width * n_req

    blocks = lax.all_gather(verify_in, ("expert", "req"), axis=0)
    blocks = blocks.reshape(n_expert, n_req, own_rows, own_width)
    hidden_in = blocks.transpose(0, 2, 1, 3).reshape(rows, width)
    routes = jnp.concatenate([expert_ids.astype(jnp.float32), gate_weights], axis=1)
    routes = lax.all_gather(routes, "expert", axis=0, tiled=True)
    top = expert_ids.shape[1]
    ids, gains = routes[:, :top].astype(jnp.int32), routes[:, top:]
    held = (lax.axis_index("expert") * local + jnp.arange(local, dtype=jnp.int32)) // slices
    mixing = jnp.sum(
        jnp.where(ids[None] == held[:, None, None], gains[None], 0.0), axis=2
    )

    batch = jnp.broadcast_to(hidden_in[None], (local, rows, width))
    gate = jnp.einsum("kmd,kdf->kmf", batch, moe_gate, preferred_element_type=jnp.float32)
    up = jnp.einsum("kmd,kdf->kmf", batch, moe_up, preferred_element_type=jnp.float32)
    hidden = (jax.nn.silu(gate) * up * mixing[:, :, None]).astype(jnp.bfloat16)
    hidden = hidden.transpose(1, 0, 2).reshape(rows, -1)
    down = moe_down.reshape(-1, width)
    partial = jnp.dot(hidden, down, preferred_element_type=jnp.float32).astype(jnp.bfloat16)
    partial = partial.reshape(n_expert, own_rows, n_req, own_width).transpose(0, 2, 1, 3)
    partial = partial.reshape(n_expert * n_req, own_rows, own_width)
    out = lax.psum_scatter(partial, ("expert", "req"), scatter_dimension=0)
    return out.astype(jnp.bfloat16)


def draft_step(
    draft_emb, draft_feat, parents, join_weight, norm_gain, draft_gate, draft_up, draft_down
):
    n_expert, n_req = lax.axis_size("expert"), lax.axis_size("req")
    n_group = lax.axis_size("group")
    r, g = lax.axis_index("req"), lax.axis_index("group")
    half = n_req // 2
    side, place = r // half, r % half
    rows, width = draft_emb.shape[0], draft_emb.shape[1] * n_expert

    def across(x):
        return lax.ppermute(x, "req", [(i, (i + half) % n_req) for i in range(n_req)])

    def within(x, step):
        return lax.ppermute(
            x,
            "req",
            [(i // half * half + (i + step) % half, i) for i in range(n_req)],
        )

    def other_group(x, step):
        return lax.ppermute(x, "group", [((i + step) % n_group, i) for i in range(n_group)])

    def pieces_of(weight):
        found = [(side * half + (place + s) % half, None, weight if s == 0 else within(weight, s))
                 for s in range(half)]
        depth = weight.shape[0] // n_group
        part = lax.dynamic_slice_in_dim(weight, g * depth, depth, axis=0)
        crossed = across(part)
        far = [(g, crossed)]
        far += [((g + s) % n_group, other_group(crossed, s)) for s in range(1, n_group)]
        for s in range(half):
            index = (1 - side) * half + (place + s) % half
            found += [(index, p, a if s == 0 else within(a, s)) for p, a in far]
        return found

    local_parent = parents - r * rows
    feat = jnp.take(draft_feat, local_parent, axis=0)
    mine = jnp.where(side == 0, draft_emb, feat)
    theirs = across(jnp.where(side == 0, feat, draft_emb))
    join_pieces = [
        ((place + s) % half, join_weight if s == 0 else within(join_weight, s))
        for s in range(half)
    ]
    depth = join_weight.shape[0]

    def join(block):
        whole = lax.all_gather(block, "expert", axis=1, tiled=True)
        return sum(
            jnp.dot(
                lax.dynamic_slice_in_dim(whole, index * depth, depth, axis=1),
                weight,
                preferred_element_type=jnp.float32,
            )
            for index, weight in join_pieces
        )

    kept = join(mine)
    sent = join(theirs)
    joined_state = kept + across(sent.astype(jnp.bfloat16)).astype(jnp.float32)

    squares = lax.psum(jnp.sum(joined_state * joined_state, axis=1), "expert")
    scale = lax.rsqrt(squares[:, None] / width + EPS)
    scaled = (joined_state * norm_gain[None, :]).astype(jnp.bfloat16)
    inputs = lax.all_gather(scaled, "expert", axis=1, tiled=True)

    def project(weight):
        total = 0.0
        full = weight.shape[0]
        for index, part, array in pieces_of(weight):
            start = index * full if part is None else index * full + part * array.shape[0]
            columns = lax.dynamic_slice_in_dim(inputs, start, array.shape[0], axis=1)
            total += jnp.dot(columns, array, preferred_element_type=jnp.float32)
        return total

    gate = project(draft_gate) * scale
    up = project(draft_up) * scale
    hidden = (jax.nn.silu(gate) * up).astype(jnp.bfloat16)

    near, far = [], []
    full = draft_down.shape[0]
    pieces = pieces_of(draft_down)
    for s in range(half):
        near.append(jnp.dot(hidden, pieces[s][2], preferred_element_type=jnp.float32))
    for s in range(half):
        total = 0.0
        for _, part, array in pieces[half + s * n_group : half + (s + 1) * n_group]:
            columns = lax.dynamic_slice_in_dim(hidden, part * array.shape[0], array.shape[0], axis=1)
            total += jnp.dot(columns, array, preferred_element_type=jnp.float32)
        far.append(total)

    def ordered(blocks):
        stack = jnp.stack(blocks).astype(jnp.bfloat16)
        order = (jnp.arange(half) - place) % half
        return stack[order]

    near, far = ordered(near), ordered(far)
    both = jnp.where(side == 0, jnp.concatenate([near, far]), jnp.concatenate([far, near]))
    terms = both.transpose(1, 0, 2).reshape(rows, width)
    mlp_sum = lax.psum_scatter(terms, "expert", scatter_dimension=1, tiled=True)
    return (joined_state + mlp_sum.astype(jnp.float32)).astype(jnp.bfloat16)


def per_device(
    verify_in,
    expert_ids,
    gate_weights,
    moe_gate,
    moe_up,
    moe_down,
    draft_emb,
    draft_feat,
    parents,
    join_weight,
    norm_gain,
    draft_gate,
    draft_up,
    draft_down,
):
    draft_out = draft_step(
        draft_emb, draft_feat, parents, join_weight, norm_gain, draft_gate, draft_up, draft_down
    )
    verify_out = verify_layer(verify_in, expert_ids, gate_weights, moe_gate, moe_up, moe_down)
    return (verify_out, draft_out)


def solution(mesh):
    in_specs = (
        P(("group", "expert"), "req"),
        P(("group", "expert"), None),
        P(("group", "expert"), None),
        P("expert", None, "req"),
        P("expert", None, "req"),
        P("expert", "req", None),
        P(("group", "req"), "expert"),
        P(("group", "req"), "expert"),
        P(("group", "req")),
        P("req", "expert"),
        P("expert"),
        P("req", "expert"),
        P("req", "expert"),
        P("expert", "req"),
    )
    out_specs = (P(("group", "expert"), "req"), P(("group", "req"), "expert"))
    return jax.shard_map(
        per_device, mesh=mesh, in_specs=in_specs, out_specs=out_specs, check_vma=False
    )
```

```python
import functools

import jax
import jax.numpy as jnp
from jax import lax
from jax.experimental import pallas as pl
from jax.experimental.pallas import tpu as pltpu
from jax.sharding import PartitionSpec as P

EXPERTS = 8
EPS = 1e-05


def verify_layer(verify_in, expert_ids, gate_weights, moe_gate, moe_up, moe_down):
    n_expert, n_req = lax.axis_size("expert"), lax.axis_size("req")
    own_rows, own_width = verify_in.shape
    local = moe_gate.shape[0]
    slices = local * n_expert // EXPERTS
    rows, width = own_rows * n_expert, own_width * n_req

    blocks = lax.all_gather(verify_in, ("expert", "req"), axis=0)
    blocks = blocks.reshape(n_expert, n_req, own_rows, own_width)
    hidden_in = blocks.transpose(0, 2, 1, 3).reshape(rows, width)
    routes = jnp.concatenate([expert_ids.astype(jnp.float32), gate_weights], axis=1)
    routes = lax.all_gather(routes, "expert", axis=0, tiled=True)
    top = expert_ids.shape[1]
    ids, gains = routes[:, :top].astype(jnp.int32), routes[:, top:]
    held = (lax.axis_index("expert") * local + jnp.arange(local, dtype=jnp.int32)) // slices
    mixing = jnp.sum(
        jnp.where(ids[None] == held[:, None, None], gains[None], 0.0), axis=2
    )

    batch = jnp.broadcast_to(hidden_in[None], (local, rows, width))
    gate = jnp.einsum("kmd,kdf->kmf", batch, moe_gate, preferred_element_type=jnp.float32)
    up = jnp.einsum("kmd,kdf->kmf", batch, moe_up, preferred_element_type=jnp.float32)
    hidden = (jax.nn.silu(gate) * up * mixing[:, :, None]).astype(jnp.bfloat16)
    hidden = hidden.transpose(1, 0, 2).reshape(rows, -1)
    down = moe_down.reshape(-1, width)
    partial = jnp.dot(hidden, down, preferred_element_type=jnp.float32).astype(jnp.bfloat16)
    partial = partial.reshape(n_expert, own_rows, n_req, own_width).transpose(0, 2, 1, 3)
    partial = partial.reshape(n_expert * n_req, own_rows, own_width)
    out = lax.psum_scatter(partial, ("expert", "req"), scatter_dimension=0)
    return out.astype(jnp.bfloat16)


def draft_step(
    draft_emb, draft_feat, parents, join_weight, norm_gain, draft_gate, draft_up, draft_down
):
    n_expert, n_req = lax.axis_size("expert"), lax.axis_size("req")
    n_group = lax.axis_size("group")
    r, g = lax.axis_index("req"), lax.axis_index("group")
    half = n_req // 2
    side, place = r // half, r % half
    rows, width = draft_emb.shape[0], draft_emb.shape[1] * n_expert

    def across(x):
        return lax.ppermute(x, "req", [(i, (i + half) % n_req) for i in range(n_req)])

    def within(x, step):
        return lax.ppermute(
            x,
            "req",
            [(i // half * half + (i + step) % half, i) for i in range(n_req)],
        )

    def other_group(x, step):
        return lax.ppermute(x, "group", [((i + step) % n_group, i) for i in range(n_group)])

    def pieces_of(weight):
        found = [(side * half + (place + s) % half, None, weight if s == 0 else within(weight, s))
                 for s in range(half)]
        depth = weight.shape[0] // n_group
        part = lax.dynamic_slice_in_dim(weight, g * depth, depth, axis=0)
        crossed = across(part)
        far = [(g, crossed)]
        far += [((g + s) % n_group, other_group(crossed, s)) for s in range(1, n_group)]
        for s in range(half):
            index = (1 - side) * half + (place + s) % half
            found += [(index, p, a if s == 0 else within(a, s)) for p, a in far]
        return found

    local_parent = parents - r * rows
    feat = jnp.take(draft_feat, local_parent, axis=0)
    mine = jnp.where(side == 0, draft_emb, feat)
    theirs = across(jnp.where(side == 0, feat, draft_emb))
    join_pieces = [
        ((place + s) % half, join_weight if s == 0 else within(join_weight, s))
        for s in range(half)
    ]
    depth = join_weight.shape[0]

    def join(block):
        whole = lax.all_gather(block, "expert", axis=1, tiled=True)
        return sum(
            jnp.dot(
                lax.dynamic_slice_in_dim(whole, index * depth, depth, axis=1),
                weight,
                preferred_element_type=jnp.float32,
            )
            for index, weight in join_pieces
        )

    kept = join(mine)
    sent = join(theirs)
    joined_state = kept + across(sent.astype(jnp.bfloat16)).astype(jnp.float32)

    squares = lax.psum(jnp.sum(joined_state * joined_state, axis=1), "expert")
    scale = lax.rsqrt(squares[:, None] / width + EPS)
    scaled = (joined_state * norm_gain[None, :]).astype(jnp.bfloat16)
    inputs = lax.all_gather(scaled, "expert", axis=1, tiled=True)

    def project(weight):
        total = 0.0
        full = weight.shape[0]
        for index, part, array in pieces_of(weight):
            start = index * full if part is None else index * full + part * array.shape[0]
            columns = lax.dynamic_slice_in_dim(inputs, start, array.shape[0], axis=1)
            total += jnp.dot(columns, array, preferred_element_type=jnp.float32)
        return total

    gate = project(draft_gate) * scale
    up = project(draft_up) * scale
    hidden = (jax.nn.silu(gate) * up).astype(jnp.bfloat16)

    near, far = [], []
    full = draft_down.shape[0]
    pieces = pieces_of(draft_down)
    for s in range(half):
        near.append(jnp.dot(hidden, pieces[s][2], preferred_element_type=jnp.float32))
    for s in range(half):
        total = 0.0
        for _, part, array in pieces[half + s * n_group : half + (s + 1) * n_group]:
            columns = lax.dynamic_slice_in_dim(hidden, part * array.shape[0], array.shape[0], axis=1)
            total += jnp.dot(columns, array, preferred_element_type=jnp.float32)
        far.append(total)

    def ordered(blocks):
        stack = jnp.stack(blocks).astype(jnp.bfloat16)
        order = (jnp.arange(half) - place) % half
        return stack[order]

    near, far = ordered(near), ordered(far)
    both = jnp.where(side == 0, jnp.concatenate([near, far]), jnp.concatenate([far, near]))
    terms = both.transpose(1, 0, 2).reshape(rows, width)
    mlp_sum = lax.psum_scatter(terms, "expert", scatter_dimension=1, tiled=True)
    return (joined_state + mlp_sum.astype(jnp.float32)).astype(jnp.bfloat16)


def front_kernel(
    shape,
    mine_ref, theirs_ref, gain_ref, rows_ref, routes_ref,
    join_ref, gate_ref, up_ref, down_ref, moe_gate_ref, moe_up_ref, moe_down_ref,
    state_ref, verify_ref, squares_ref, scaled_ref,
    gate_sib, up_sib, down_sib, gate_far, up_far, down_far, gate_sibfar, up_sibfar, down_sibfar,
    near_all, far_all, near_acc, sent_acc, swap_out, swap_in, join_all, square_buf, scaled_buf,
    row_all, route_all, gate_buf, up_buf, down_buf, moe_acc, moe_out, moe_in, merged_out, merged_in,
    ring_send_r, ring_send_l, ring_recv, misc_send, misc_recv, local_sem, moe_sem,
    mate_send, mate_recv, wide_send, wide_recv,
):
    n_expert, n_req, n_group, slices = shape
    half = n_req // 2
    g, e, r = lax.axis_index("group"), lax.axis_index("expert"), lax.axis_index("req")
    place = lax.rem(r, half)
    sib = r + 1 - 2 * place
    partner = lax.rem(r + half, n_req)

    def remote(src, dst, send, recv, **where):
        return pltpu.make_async_remote_copy(
            src_ref=src, dst_ref=dst, send_sem=send, recv_sem=recv,
            device_id=where, device_id_type=pl.DeviceIdType.MESH,
        )

    barrier = pltpu.get_barrier_semaphore()
    for s in range(1, n_req):
        pl.semaphore_signal(barrier, inc=1, device_id={"req": lax.rem(r + s, n_req)},
                            device_id_type=pl.DeviceIdType.MESH)
    for s in range(1, n_expert):
        pl.semaphore_signal(barrier, inc=1, device_id={"expert": lax.rem(e + s, n_expert)},
                            device_id_type=pl.DeviceIdType.MESH)
    pl.semaphore_signal(barrier, inc=1, device_id={"group": 1 - g},
                        device_id_type=pl.DeviceIdType.MESH)

    local = moe_gate_ref.shape[0]

    def fetch(k, slot):
        return [
            pltpu.make_async_copy(w.at[k], b.at[slot], moe_sem.at[i, slot])
            for i, (w, b) in enumerate(
                ((moe_gate_ref, gate_buf), (moe_up_ref, up_buf), (moe_down_ref, down_buf)))
        ]

    for c in fetch(0, 0):
        c.start()
    own_join = pltpu.make_async_copy(join_ref, join_all.at[place], local_sem.at[0])
    own_join.start()
    own_width = rows_ref.shape[1]
    own_columns = pl.ds(pl.multiple_of(r * own_width, own_width), own_width)
    near_all[e] = mine_ref[...]
    row_all[e, :, own_columns] = rows_ref[...]
    route_all[e] = routes_ref[...]
    pl.semaphore_wait(barrier, n_req + n_expert - 1)

    def to_right(i, buf, b):
        return remote(buf.at[b], buf.at[b], ring_send_r.at[i, b], ring_recv.at[i, b],
                      expert=lax.rem(e + 1, n_expert))

    def to_left(i, buf, b):
        return remote(buf.at[b], buf.at[b], ring_send_l.at[i, b], ring_recv.at[i, b],
                      expert=lax.rem(e + n_expert - 1, n_expert))

    def ring_start(i, buf):
        @pl.when(e < n_expert - 1)
        def _():
            to_right(i, buf, e).start()

        @pl.when(e > 0)
        def _():
            to_left(i, buf, e).start()

    def ring_step(i, buf, s):
        @pl.when(e >= s)
        def _():
            to_right(i, buf, e - s).wait_recv()

            @pl.when(e < n_expert - 1)
            def _():
                to_right(i, buf, e - s).start()

        @pl.when(e + s < n_expert)
        def _():
            to_left(i, buf, e + s).wait_recv()

            @pl.when(e > 0)
            def _():
                to_left(i, buf, e + s).start()

    def ring_finish(i, buf):
        for b in range(n_expert):
            @pl.when((b <= e) & (e < n_expert - 1))
            def _():
                to_right(i, buf, b).wait_send()

            @pl.when((b >= e) & (e > 0))
            def _():
                to_left(i, buf, b).wait_send()

    def mates(buf_of, dst_of, row, axis, me, n):
        copies = []
        for s in range(1, n):
            mate = lax.rem(me + s, n)
            c = remote(buf_of(mate), dst_of, mate_send.at[row, s], mate_recv.at[row, s], **{axis: mate})
            c.start()
            copies.append(c)
        return copies

    cross = remote(theirs_ref, far_all.at[e], misc_send.at[0], misc_recv.at[0], req=partner)
    cross.start()
    rows_req = mates(lambda m: rows_ref, row_all.at[e, :, own_columns], 0, "req", r, n_req)
    routes_out = mates(lambda m: routes_ref, route_all.at[e], 1, "expert", e, n_expert)
    ring_start(0, near_all)
    join_out = remote(join_ref, join_all.at[place], misc_send.at[1], misc_recv.at[1], req=sib)
    join_out.start()
    for c in rows_req:
        c.wait_recv()
    rows_exp = mates(lambda m: row_all.at[e], row_all.at[e], 2, "expert", e, n_expert)
    sib_out = []
    for i, (w, d) in enumerate(((gate_ref, gate_sib), (up_ref, up_sib), (down_ref, down_sib))):
        c = remote(w, d, misc_send.at[2 + i], misc_recv.at[2 + i], req=sib)
        c.start()
        sib_out.append(c)

    weights = ((gate_ref, gate_far, gate_sibfar), (up_ref, up_far, up_sibfar), (down_ref, down_far, down_sibfar))
    cuts = 2
    chunks = []
    for own, far, sibfar in weights:
        part = own.shape[0] // n_group
        piece = part // cuts
        for cut in range(cuts):
            chunks.append((own, far, sibfar, part, piece, cut * piece))

    def span(c, owner):
        _, _, _, part, piece, start = chunks[c]
        return pl.ds(pl.multiple_of(owner * part + start, 16), piece)

    def over_req(c):
        at = span(c, g)
        return remote(chunks[c][0].at[at], chunks[c][1].at[at], wide_send.at[0, c], wide_recv.at[0, c], req=partner)

    def over_group(c):
        at = span(c, g)
        return remote(chunks[c][1].at[at], chunks[c][1].at[at], wide_send.at[1, c], wide_recv.at[1, c], group=1 - g)

    def to_sib(c, which):
        at = span(c, g if which == 2 else 1 - g)
        return remote(chunks[c][1].at[at], chunks[c][2].at[at], wide_send.at[which, c], wide_recv.at[which, c], req=sib)

    count = len(chunks)

    def relay(c):
        over_req(c).wait_recv()
        if c + 2 < count:
            over_req(c + 2).start()
        over_group(c).start()
        to_sib(c, 2).start()
        if c > 0:
            relay_last(c - 1)

    def relay_last(c):
        over_group(c).wait_recv()
        to_sib(c, 3).start()

    cross.wait_recv()
    ring_start(1, far_all)
    over_req(0).start()
    over_req(1).start()
    ring_step(0, near_all, 1)
    for c in rows_exp + routes_out:
        c.wait_recv()
    moe_acc[...] = jnp.zeros_like(moe_acc)
    own_rows = rows_ref.shape[0]
    rows = own_rows * n_expert

    def expert_piece(k, carry):
        slot = lax.rem(k, 2)

        @pl.when(k + 1 < local)
        def _():
            for c in fetch(k + 1, 1 - slot):
                c.start()

        for c in fetch(k, slot):
            c.wait()
        x = row_all[...].reshape(rows, row_all.shape[2])
        routes = route_all[...].reshape(rows, route_all.shape[2])
        expert = ((e * local + k) // slices).astype(jnp.float32)
        mixing = jnp.where(routes[:, 0:1] == expert, routes[:, 2:3], 0.0)
        mixing += jnp.where(routes[:, 1:2] == expert, routes[:, 3:4], 0.0)
        a = jnp.dot(x, gate_buf[slot], preferred_element_type=jnp.float32)
        b = jnp.dot(x, up_buf[slot], preferred_element_type=jnp.float32)
        hidden = (a / (1.0 + jnp.exp(-a)) * b * mixing).astype(jnp.bfloat16)
        moe_acc[...] += jnp.dot(hidden, down_buf[slot], preferred_element_type=jnp.float32)
        return carry

    def moe(start, stop):
        lax.fori_loop(start, stop, expert_piece, 0)

    quarter = local // 4
    moe(0, quarter)
    ring_step(0, near_all, 2)
    ring_step(1, far_all, 1)
    moe(quarter, 2 * quarter)
    relay(0)
    ring_step(0, near_all, 3)
    moe(2 * quarter, 3 * quarter)
    ring_step(1, far_all, 2)
    moe(3 * quarter, local)
    relay(1)

    moe_out[...] = moe_acc[...].astype(jnp.bfloat16).reshape(moe_out.shape)
    merge_exp = mates(lambda m: moe_out.at[m], moe_in.at[e], 3, "expert", e, n_expert)

    own_join.wait()
    join_out.wait_recv()
    block = near_all.shape[2]
    per = join_ref.shape[0] // block
    tile = 256

    def join(buf, acc):
        for n in range(acc.shape[1] // tile):
            at = pl.ds(n * tile, tile)
            total = 0.0
            for b in range(n_expert):
                w = join_all[b // per, pl.ds(b % per * block, block), at]
                total += jnp.dot(buf[b], w, preferred_element_type=jnp.float32)
            acc[:, at] = total

    join(near_all, near_acc)
    ring_step(1, far_all, 3)
    join(far_all, sent_acc)
    swap_out[...] = sent_acc[...].astype(jnp.bfloat16)
    swap = remote(swap_out, swap_in, misc_send.at[5], misc_recv.at[5], req=partner)
    swap.start()

    for c in merge_exp:
        c.wait_recv()
    merged = moe_out[e].astype(jnp.float32)
    for s in range(1, n_expert):
        merged += moe_in[lax.rem(e + n_expert - s, n_expert)].astype(jnp.float32)
    for j in range(n_req):
        merged_out[j] = merged[:, j * own_width:(j + 1) * own_width].astype(jnp.bfloat16)
    merge_req = mates(lambda m: merged_out.at[m], merged_in.at[r], 4, "req", r, n_req)

    swap.wait_recv()
    state = near_acc[...] + swap_in[...].astype(jnp.float32)
    state_ref[...] = state
    scaled_buf[e] = (state * gain_ref[...]).astype(jnp.bfloat16)
    ring_start(2, scaled_buf)
    lane = lax.broadcasted_iota(jnp.int32, (128, 128), 1)
    line = lax.broadcasted_iota(jnp.int32, (128, 128), 0)
    sums = jnp.sum(state * state, axis=1, keepdims=True)
    for j in range(state.shape[0] // 128):
        picked = jnp.where(lane == line, sums[j * 128:(j + 1) * 128], 0.0)
        square_buf[e, j:j + 1, :] = jnp.sum(picked, axis=0, keepdims=True)
    squares_out = mates(lambda m: square_buf.at[e], square_buf.at[e], 5, "expert", e, n_expert)

    for c in merge_req:
        c.wait_recv()
    out = merged_out[r].astype(jnp.float32)
    for s in range(1, n_req):
        out += merged_in[lax.rem(r + n_req - s, n_req)].astype(jnp.float32)
    verify_ref[...] = out.astype(jnp.bfloat16)

    relay(2)
    ring_step(2, scaled_buf, 1)
    relay(3)
    ring_step(2, scaled_buf, 2)
    relay(4)
    ring_step(2, scaled_buf, 3)
    for c in squares_out:
        c.wait_recv()
    squares_ref[...] = square_buf[...]
    keep = pltpu.make_async_copy(scaled_buf, scaled_ref, local_sem.at[1])
    keep.start()
    relay(5)
    relay_last(count - 1)
    keep.wait()

    for c in rows_req + routes_out + rows_exp + merge_exp + merge_req + squares_out + sib_out:
        c.wait_send()
    for c in (cross, join_out, swap):
        c.wait_send()
    for c in sib_out:
        c.wait_recv()
    for i, buf in enumerate((near_all, far_all, scaled_buf)):
        ring_finish(i, buf)
    for c in range(count):
        over_req(c).wait_send()
        over_group(c).wait_send()
        to_sib(c, 2).wait()
        to_sib(c, 3).wait()


def front(
    mine, theirs, gain, verify_in, routes, join_weight, draft_gate, draft_up, draft_down,
    moe_gate, moe_up, moe_down,
):
    n_expert, n_req, n_group = (lax.axis_size(a) for a in ("expert", "req", "group"))
    local, width, ff = moe_gate.shape
    slices = local * n_expert // EXPERTS
    rows, block = mine.shape
    own_rows, own_width = verify_in.shape
    bf, f32 = jnp.bfloat16, jnp.float32
    vmem, hbm = pl.BlockSpec(memory_space=pltpu.VMEM), pl.BlockSpec(memory_space=pl.ANY)
    weights = (draft_gate, draft_up, draft_down)
    like = [jax.ShapeDtypeStruct(w.shape, w.dtype) for w in weights]
    dma = pltpu.SemaphoreType.DMA
    n_chunks = 6
    big = max(n_expert, n_req)
    return pl.pallas_call(
        functools.partial(front_kernel, (n_expert, n_req, n_group, slices)),
        out_shape=[
            jax.ShapeDtypeStruct((rows, block), f32),
            jax.ShapeDtypeStruct(verify_in.shape, bf),
            jax.ShapeDtypeStruct((n_expert, 8, 128), f32),
            jax.ShapeDtypeStruct((n_expert, rows, block), bf),
            *like, *like, *like,
        ],
        in_specs=[vmem] * 5 + [hbm] * 7,
        out_specs=[vmem] * 3 + [hbm] * 10,
        scratch_shapes=[
            pltpu.VMEM((n_expert, rows, block), bf),
            pltpu.VMEM((n_expert, rows, block), bf),
            pltpu.VMEM((rows, block), f32),
            pltpu.VMEM((rows, block), f32),
            pltpu.VMEM((rows, block), bf),
            pltpu.VMEM((rows, block), bf),
            pltpu.VMEM((n_req // 2, *join_weight.shape), bf),
            pltpu.VMEM((n_expert, 8, 128), f32),
            pltpu.VMEM((n_expert, rows, block), bf),
            pltpu.VMEM((n_expert, own_rows, width), bf),
            pltpu.VMEM((n_expert, *routes.shape), f32),
            pltpu.VMEM((2, width, ff), bf),
            pltpu.VMEM((2, width, ff), bf),
            pltpu.VMEM((2, ff, width), bf),
            pltpu.VMEM((n_expert * own_rows, width), f32),
            pltpu.VMEM((n_expert, own_rows, width), bf),
            pltpu.VMEM((n_expert, own_rows, width), bf),
            pltpu.VMEM((n_req, own_rows, own_width), bf),
            pltpu.VMEM((n_req, own_rows, own_width), bf),
            dma((3, n_expert)), dma((3, n_expert)), dma((3, n_expert)),
            dma((6,)), dma((6,)), dma((2,)), dma((3, 2)),
            dma((6, big)), dma((6, big)), dma((4, n_chunks)), dma((4, n_chunks)),
        ],
        compiler_params=pltpu.CompilerParams(
            collective_id=0, has_side_effects=True, vmem_limit_bytes=56 * 2**20
        ),
        name="front",
    )(mine, theirs, gain, verify_in, routes, join_weight, *weights, moe_gate, moe_up, moe_down)


def fused(
    verify_in, expert_ids, gate_weights, moe_gate, moe_up, moe_down,
    draft_emb, draft_feat, parents, join_weight, norm_gain, draft_gate, draft_up, draft_down,
):
    n_expert, n_req = lax.axis_size("expert"), lax.axis_size("req")
    r = lax.axis_index("req")
    half = n_req // 2
    side, place = r // half, r % half
    rows, width = draft_emb.shape[0], draft_emb.shape[1] * n_expert
    feat = jnp.take(draft_feat, parents - r * rows, axis=0)
    mine = jnp.where(side == 0, draft_emb, feat)
    theirs = jnp.where(side == 0, feat, draft_emb)
    routes = jnp.concatenate([expert_ids.astype(jnp.float32), gate_weights], axis=1)
    routes = jnp.pad(routes, ((0, 0), (0, 128 - routes.shape[1])))
    state, verify_out, squares, inputs, *moved = front(
        mine, theirs, norm_gain[None, :], verify_in, routes, join_weight,
        draft_gate, draft_up, draft_down, moe_gate, moe_up, moe_down,
    )
    squares = jnp.sum(squares, axis=0).reshape(-1)[:rows]
    scale = lax.rsqrt(squares[:, None] / width + EPS)
    sib, partner = side * half + (1 - place), (r + half) % n_req
    sibfar = partner + 1 - 2 * place
    places = (r, sib, partner, sibfar)
    per_gate, per_up, per_down = (
        [w, moved[i], moved[3 + i], moved[6 + i]]
        for i, w in enumerate((draft_gate, draft_up, draft_down))
    )
    columns = [lax.dynamic_index_in_dim(inputs, p, 0, keepdims=False) for p in places]

    def project(shards):
        return scale * sum(
            jnp.dot(c, w, preferred_element_type=jnp.float32) for c, w in zip(columns, shards)
        )

    hidden = (jax.nn.silu(project(per_gate)) * project(per_up)).astype(jnp.bfloat16)
    near0, near1, far0, far1 = (
        jnp.dot(hidden, w, preferred_element_type=jnp.float32).astype(jnp.bfloat16)
        for w in per_down
    )
    n0, n1 = jnp.where(place == 0, near0, near1), jnp.where(place == 0, near1, near0)
    f0, f1 = jnp.where(place == 0, far0, far1), jnp.where(place == 0, far1, far0)
    first = jnp.where(side == 0, n0, f0), jnp.where(side == 0, n1, f1)
    second = jnp.where(side == 0, f0, n0), jnp.where(side == 0, f1, n1)
    terms = jnp.concatenate([*first, *second], axis=1)
    mlp_sum = lax.psum_scatter(terms, "expert", scatter_dimension=1, tiled=True)
    return (verify_out, (state + mlp_sum.astype(jnp.float32)).astype(jnp.bfloat16))


def per_device(
    verify_in,
    expert_ids,
    gate_weights,
    moe_gate,
    moe_up,
    moe_down,
    draft_emb,
    draft_feat,
    parents,
    join_weight,
    norm_gain,
    draft_gate,
    draft_up,
    draft_down,
):
    n_expert, n_req = lax.axis_size("expert"), lax.axis_size("req")
    block, rows = draft_emb.shape[1], draft_emb.shape[0]
    fits = (
        n_req == 4 and lax.axis_size("group") == 2 and n_expert == 4
        and join_weight.shape[0] % block == 0 and draft_gate.shape[0] == block
        and block % 256 == 0 and draft_gate.shape[1] % 128 == 0
        and rows % 128 == 0 and rows <= 1024 and expert_ids.shape[1] == 2
        and moe_gate.shape[0] % 4 == 0 and draft_down.shape[0] % 64 == 0
    )
    if fits:
        return fused(
            verify_in, expert_ids, gate_weights, moe_gate, moe_up, moe_down,
            draft_emb, draft_feat, parents, join_weight, norm_gain,
            draft_gate, draft_up, draft_down,
        )
    draft_out = draft_step(
        draft_emb, draft_feat, parents, join_weight, norm_gain, draft_gate, draft_up, draft_down
    )
    verify_out = verify_layer(verify_in, expert_ids, gate_weights, moe_gate, moe_up, moe_down)
    return (verify_out, draft_out)


def solution(mesh):
    in_specs = (
        P(("group", "expert"), "req"),
        P(("group", "expert"), None),
        P(("group", "expert"), None),
        P("expert", None, "req"),
        P("expert", None, "req"),
        P("expert", "req", None),
        P(("group", "req"), "expert"),
        P(("group", "req"), "expert"),
        P(("group", "req")),
        P("req", "expert"),
        P("expert"),
        P("req", "expert"),
        P("req", "expert"),
        P("expert", "req"),
    )
    out_specs = (P(("group", "expert"), "req"), P(("group", "req"), "expert"))
    return jax.shard_map(
        per_device, mesh=mesh, in_specs=in_specs, out_specs=out_specs, check_vma=False
    )
```

```python
import functools

import jax
import jax.numpy as jnp
from jax import lax
from jax.experimental import pallas as pl
from jax.experimental.pallas import tpu as pltpu
from jax.sharding import PartitionSpec as P

EXPERTS = 8
EPS = 1e-05
CUTS = 4
AHEAD = 4


def verify_layer(verify_in, expert_ids, gate_weights, moe_gate, moe_up, moe_down):
    n_expert, n_req = lax.axis_size("expert"), lax.axis_size("req")
    own_rows, own_width = verify_in.shape
    local = moe_gate.shape[0]
    slices = local * n_expert // EXPERTS
    rows, width = own_rows * n_expert, own_width * n_req

    blocks = lax.all_gather(verify_in, ("expert", "req"), axis=0)
    blocks = blocks.reshape(n_expert, n_req, own_rows, own_width)
    hidden_in = blocks.transpose(0, 2, 1, 3).reshape(rows, width)
    routes = jnp.concatenate([expert_ids.astype(jnp.float32), gate_weights], axis=1)
    routes = lax.all_gather(routes, "expert", axis=0, tiled=True)
    top = expert_ids.shape[1]
    ids, gains = routes[:, :top].astype(jnp.int32), routes[:, top:]
    held = (lax.axis_index("expert") * local + jnp.arange(local, dtype=jnp.int32)) // slices
    mixing = jnp.sum(
        jnp.where(ids[None] == held[:, None, None], gains[None], 0.0), axis=2
    )

    batch = jnp.broadcast_to(hidden_in[None], (local, rows, width))
    gate = jnp.einsum("kmd,kdf->kmf", batch, moe_gate, preferred_element_type=jnp.float32)
    up = jnp.einsum("kmd,kdf->kmf", batch, moe_up, preferred_element_type=jnp.float32)
    hidden = (jax.nn.silu(gate) * up * mixing[:, :, None]).astype(jnp.bfloat16)
    hidden = hidden.transpose(1, 0, 2).reshape(rows, -1)
    down = moe_down.reshape(-1, width)
    partial = jnp.dot(hidden, down, preferred_element_type=jnp.float32).astype(jnp.bfloat16)
    partial = partial.reshape(n_expert, own_rows, n_req, own_width).transpose(0, 2, 1, 3)
    partial = partial.reshape(n_expert * n_req, own_rows, own_width)
    out = lax.psum_scatter(partial, ("expert", "req"), scatter_dimension=0)
    return out.astype(jnp.bfloat16)


def draft_step(
    draft_emb, draft_feat, parents, join_weight, norm_gain, draft_gate, draft_up, draft_down
):
    n_expert, n_req = lax.axis_size("expert"), lax.axis_size("req")
    n_group = lax.axis_size("group")
    r, g = lax.axis_index("req"), lax.axis_index("group")
    half = n_req // 2
    side, place = r // half, r % half
    rows, width = draft_emb.shape[0], draft_emb.shape[1] * n_expert

    def across(x):
        return lax.ppermute(x, "req", [(i, (i + half) % n_req) for i in range(n_req)])

    def within(x, step):
        return lax.ppermute(
            x,
            "req",
            [(i // half * half + (i + step) % half, i) for i in range(n_req)],
        )

    def other_group(x, step):
        return lax.ppermute(x, "group", [((i + step) % n_group, i) for i in range(n_group)])

    def pieces_of(weight):
        found = [(side * half + (place + s) % half, None, weight if s == 0 else within(weight, s))
                 for s in range(half)]
        depth = weight.shape[0] // n_group
        part = lax.dynamic_slice_in_dim(weight, g * depth, depth, axis=0)
        crossed = across(part)
        far = [(g, crossed)]
        far += [((g + s) % n_group, other_group(crossed, s)) for s in range(1, n_group)]
        for s in range(half):
            index = (1 - side) * half + (place + s) % half
            found += [(index, p, a if s == 0 else within(a, s)) for p, a in far]
        return found

    local_parent = parents - r * rows
    feat = jnp.take(draft_feat, local_parent, axis=0)
    mine = jnp.where(side == 0, draft_emb, feat)
    theirs = across(jnp.where(side == 0, feat, draft_emb))
    join_pieces = [
        ((place + s) % half, join_weight if s == 0 else within(join_weight, s))
        for s in range(half)
    ]
    depth = join_weight.shape[0]

    def join(block):
        whole = lax.all_gather(block, "expert", axis=1, tiled=True)
        return sum(
            jnp.dot(
                lax.dynamic_slice_in_dim(whole, index * depth, depth, axis=1),
                weight,
                preferred_element_type=jnp.float32,
            )
            for index, weight in join_pieces
        )

    kept = join(mine)
    sent = join(theirs)
    joined_state = kept + across(sent.astype(jnp.bfloat16)).astype(jnp.float32)

    squares = lax.psum(jnp.sum(joined_state * joined_state, axis=1), "expert")
    scale = lax.rsqrt(squares[:, None] / width + EPS)
    scaled = (joined_state * norm_gain[None, :]).astype(jnp.bfloat16)
    inputs = lax.all_gather(scaled, "expert", axis=1, tiled=True)

    def project(weight):
        total = 0.0
        full = weight.shape[0]
        for index, part, array in pieces_of(weight):
            start = index * full if part is None else index * full + part * array.shape[0]
            columns = lax.dynamic_slice_in_dim(inputs, start, array.shape[0], axis=1)
            total += jnp.dot(columns, array, preferred_element_type=jnp.float32)
        return total

    gate = project(draft_gate) * scale
    up = project(draft_up) * scale
    hidden = (jax.nn.silu(gate) * up).astype(jnp.bfloat16)

    near, far = [], []
    full = draft_down.shape[0]
    pieces = pieces_of(draft_down)
    for s in range(half):
        near.append(jnp.dot(hidden, pieces[s][2], preferred_element_type=jnp.float32))
    for s in range(half):
        total = 0.0
        for _, part, array in pieces[half + s * n_group : half + (s + 1) * n_group]:
            columns = lax.dynamic_slice_in_dim(hidden, part * array.shape[0], array.shape[0], axis=1)
            total += jnp.dot(columns, array, preferred_element_type=jnp.float32)
        far.append(total)

    def ordered(blocks):
        stack = jnp.stack(blocks).astype(jnp.bfloat16)
        order = (jnp.arange(half) - place) % half
        return stack[order]

    near, far = ordered(near), ordered(far)
    both = jnp.where(side == 0, jnp.concatenate([near, far]), jnp.concatenate([far, near]))
    terms = both.transpose(1, 0, 2).reshape(rows, width)
    mlp_sum = lax.psum_scatter(terms, "expert", scatter_dimension=1, tiled=True)
    return (joined_state + mlp_sum.astype(jnp.float32)).astype(jnp.bfloat16)


def whole_kernel(
    shape,
    mine_ref, theirs_ref, gain_ref, rows_ref, routes_ref,
    join_ref, gate_ref, up_ref, down_ref, moe_gate_ref, moe_up_ref, moe_down_ref,
    verify_ref, out_ref,
    gate_sib, up_sib, down_sib, gate_far, up_far, down_far, gate_sibfar, up_sibfar, down_sibfar,
    near_all, far_all, near_acc, sent_acc, swap_out, swap_in, join_all, square_buf, scaled_buf,
    row_all, route_all, gate_buf, up_buf, down_buf, moe_acc, moe_out, moe_in, merged_out, merged_in,
    ring_send_r, ring_send_l, ring_recv, misc_send, misc_recv, local_sem, moe_sem,
    mate_send, mate_recv, wide_send, wide_recv,
    gate_acc, up_acc, hidden_buf, sum_in, stream_sem, sum_send, sum_recv,
):
    n_expert, n_req, n_group, slices = shape
    half = n_req // 2
    g, e, r = lax.axis_index("group"), lax.axis_index("expert"), lax.axis_index("req")
    place = lax.rem(r, half)
    sib = r + 1 - 2 * place
    partner = lax.rem(r + half, n_req)

    def remote(src, dst, send, recv, **where):
        return pltpu.make_async_remote_copy(
            src_ref=src, dst_ref=dst, send_sem=send, recv_sem=recv,
            device_id=where, device_id_type=pl.DeviceIdType.MESH,
        )

    barrier = pltpu.get_barrier_semaphore()
    for s in range(1, n_req):
        pl.semaphore_signal(barrier, inc=1, device_id={"req": lax.rem(r + s, n_req)},
                            device_id_type=pl.DeviceIdType.MESH)
    for s in range(1, n_expert):
        pl.semaphore_signal(barrier, inc=1, device_id={"expert": lax.rem(e + s, n_expert)},
                            device_id_type=pl.DeviceIdType.MESH)
    pl.semaphore_signal(barrier, inc=1, device_id={"group": 1 - g},
                        device_id_type=pl.DeviceIdType.MESH)

    local = moe_gate_ref.shape[0]

    def fetch(k, slot):
        return [
            pltpu.make_async_copy(w.at[k], b.at[slot], moe_sem.at[i, slot])
            for i, (w, b) in enumerate(
                ((moe_gate_ref, gate_buf), (moe_up_ref, up_buf), (moe_down_ref, down_buf)))
        ]

    for c in fetch(0, 0):
        c.start()
    own_join = pltpu.make_async_copy(join_ref, join_all.at[place], local_sem.at[0])
    own_join.start()
    own_width = rows_ref.shape[1]
    own_columns = pl.ds(pl.multiple_of(r * own_width, own_width), own_width)
    near_all[e] = mine_ref[...]
    row_all[e, :, own_columns] = rows_ref[...]
    route_all[e] = routes_ref[...]
    pl.semaphore_wait(barrier, n_req + n_expert - 1)

    def to_right(i, buf, b):
        return remote(buf.at[b], buf.at[b], ring_send_r.at[i, b], ring_recv.at[i, b],
                      expert=lax.rem(e + 1, n_expert))

    def to_left(i, buf, b):
        return remote(buf.at[b], buf.at[b], ring_send_l.at[i, b], ring_recv.at[i, b],
                      expert=lax.rem(e + n_expert - 1, n_expert))

    def ring_start(i, buf):
        @pl.when(e < n_expert - 1)
        def _():
            to_right(i, buf, e).start()

        @pl.when(e > 0)
        def _():
            to_left(i, buf, e).start()

    def ring_step(i, buf, s):
        @pl.when(e >= s)
        def _():
            to_right(i, buf, e - s).wait_recv()

            @pl.when(e < n_expert - 1)
            def _():
                to_right(i, buf, e - s).start()

        @pl.when(e + s < n_expert)
        def _():
            to_left(i, buf, e + s).wait_recv()

            @pl.when(e > 0)
            def _():
                to_left(i, buf, e + s).start()

    def ring_finish(i, buf):
        for b in range(n_expert):
            @pl.when((b <= e) & (e < n_expert - 1))
            def _():
                to_right(i, buf, b).wait_send()

            @pl.when((b >= e) & (e > 0))
            def _():
                to_left(i, buf, b).wait_send()

    def mates(buf_of, dst_of, row, axis, me, n):
        copies = []
        for s in range(1, n):
            mate = lax.rem(me + s, n)
            c = remote(buf_of(mate), dst_of, mate_send.at[row, s], mate_recv.at[row, s], **{axis: mate})
            c.start()
            copies.append(c)
        return copies

    cross = remote(theirs_ref, far_all.at[e], misc_send.at[0], misc_recv.at[0], req=partner)
    cross.start()
    rows_req = mates(lambda m: rows_ref, row_all.at[e, :, own_columns], 0, "req", r, n_req)
    routes_out = mates(lambda m: routes_ref, route_all.at[e], 1, "expert", e, n_expert)
    ring_start(0, near_all)
    join_out = remote(join_ref, join_all.at[place], misc_send.at[1], misc_recv.at[1], req=sib)
    join_out.start()
    for c in rows_req:
        c.wait_recv()
    rows_exp = mates(lambda m: row_all.at[e], row_all.at[e], 2, "expert", e, n_expert)
    sib_out = []
    for i, (w, d) in enumerate(((gate_ref, gate_sib), (up_ref, up_sib), (down_ref, down_sib))):
        c = remote(w, d, misc_send.at[2 + i], misc_recv.at[2 + i], req=sib)
        c.start()
        sib_out.append(c)

    weights = ((gate_ref, gate_far, gate_sibfar), (up_ref, up_far, up_sibfar), (down_ref, down_far, down_sibfar))
    cuts = CUTS
    chunks = []
    for own, far, sibfar in weights:
        part = own.shape[0] // n_group
        piece = part // cuts
        for cut in range(cuts):
            chunks.append((own, far, sibfar, part, piece, cut * piece))

    def span(c, owner):
        _, _, _, part, piece, start = chunks[c]
        return pl.ds(pl.multiple_of(owner * part + start, 16), piece)

    def over_req(c):
        at = span(c, g)
        return remote(chunks[c][0].at[at], chunks[c][1].at[at], wide_send.at[0, c], wide_recv.at[0, c], req=partner)

    def over_group(c):
        at = span(c, g)
        return remote(chunks[c][1].at[at], chunks[c][1].at[at], wide_send.at[1, c], wide_recv.at[1, c], group=1 - g)

    def to_sib(c, which):
        at = span(c, g if which == 2 else 1 - g)
        return remote(chunks[c][1].at[at], chunks[c][2].at[at], wide_send.at[which, c], wide_recv.at[which, c], req=sib)

    count = len(chunks)

    def relay(c):
        over_req(c).wait_recv()
        if c + AHEAD < count:
            over_req(c + AHEAD).start()
        over_group(c).start()
        to_sib(c, 2).start()
        if c > 0:
            relay_last(c - 1)

    def relay_last(c):
        over_group(c).wait_recv()
        to_sib(c, 3).start()

    cross.wait_recv()
    ring_start(1, far_all)
    for c in range(AHEAD):
        over_req(c).start()
    ring_step(0, near_all, 1)
    for c in rows_exp + routes_out:
        c.wait_recv()
    moe_acc[...] = jnp.zeros_like(moe_acc)
    own_rows = rows_ref.shape[0]
    rows = own_rows * n_expert

    def tiled(width, size, body):
        def step(n, carry):
            body(pl.ds(pl.multiple_of(n * size, size), size))
            return carry

        lax.fori_loop(0, width // size, step, 0)

    def expert_piece(k, carry):
        slot = lax.rem(k, 2)

        @pl.when(k + 1 < local)
        def _():
            for c in fetch(k + 1, 1 - slot):
                c.start()

        for c in fetch(k, slot):
            c.wait()
        x = row_all[...].reshape(rows, row_all.shape[2])
        routes = route_all[...].reshape(rows, route_all.shape[2])
        expert = ((e * local + k) // slices).astype(jnp.float32)
        mixing = jnp.where(routes[:, 0:1] == expert, routes[:, 2:3], 0.0)
        mixing += jnp.where(routes[:, 1:2] == expert, routes[:, 3:4], 0.0)
        last = (((1,), (1,)), ((), ()))
        a = lax.dot_general(x, gate_buf[slot], last, preferred_element_type=jnp.float32)
        b = lax.dot_general(x, up_buf[slot], last, preferred_element_type=jnp.float32)
        hidden = (a / (1.0 + jnp.exp(-a)) * b * mixing).astype(jnp.bfloat16)

        def columns(at):
            moe_acc[:, at] += jnp.dot(hidden, down_buf[slot, :, at], preferred_element_type=jnp.float32)

        tiled(row_all.shape[2], 512, columns)
        return carry

    def moe(start, stop):
        lax.fori_loop(start, stop, expert_piece, 0)

    quarter = local // 4
    moe(0, quarter)
    ring_step(0, near_all, 2)
    ring_step(1, far_all, 1)
    moe(quarter, 2 * quarter)
    relay(0)
    ring_step(0, near_all, 3)
    moe(2 * quarter, 3 * quarter)
    relay(1)
    ring_step(1, far_all, 2)
    moe(3 * quarter, local)
    relay(2)

    moe_out[...] = moe_acc[...].astype(jnp.bfloat16).reshape(moe_out.shape)
    merge_exp = mates(lambda m: moe_out.at[m], moe_in.at[e], 3, "expert", e, n_expert)

    own_join.wait()
    join_out.wait_recv()
    block = near_all.shape[2]
    per = join_ref.shape[0] // block
    tile = 256

    def join(buf, acc):
        def columns(at):
            total = 0.0
            for b in range(n_expert):
                w = join_all[b // per, pl.ds(b % per * block, block), at]
                total += jnp.dot(buf[b], w, preferred_element_type=jnp.float32)
            acc[:, at] = total

        tiled(acc.shape[1], tile, columns)

    relay(3)
    join(near_all, near_acc)
    relay(4)
    ring_step(1, far_all, 3)
    join(far_all, sent_acc)
    swap_out[...] = sent_acc[...].astype(jnp.bfloat16)
    swap = remote(swap_out, swap_in, misc_send.at[5], misc_recv.at[5], req=partner)
    swap.start()

    relay(5)
    for c in merge_exp:
        c.wait_recv()
    merged = moe_out[e].astype(jnp.float32)
    for s in range(1, n_expert):
        merged += moe_in[lax.rem(e + n_expert - s, n_expert)].astype(jnp.float32)
    for j in range(n_req):
        merged_out[j] = merged[:, j * own_width:(j + 1) * own_width].astype(jnp.bfloat16)
    merge_req = mates(lambda m: merged_out.at[m], merged_in.at[r], 4, "req", r, n_req)

    swap.wait_recv()
    height = near_acc.shape[0]
    sums = jnp.zeros((height, 1), jnp.float32)
    for n in range(block // tile):
        at = pl.ds(n * tile, tile)
        state = near_acc[:, at] + swap_in[:, at].astype(jnp.float32)
        near_acc[:, at] = state
        scaled_buf[e, :, at] = (state * gain_ref[:, at]).astype(jnp.bfloat16)
        sums += jnp.sum(state * state, axis=1, keepdims=True)
    ring_start(2, scaled_buf)
    lane = lax.broadcasted_iota(jnp.int32, (128, 128), 1)
    line = lax.broadcasted_iota(jnp.int32, (128, 128), 0)
    for j in range(height // 128):
        picked = jnp.where(lane == line, sums[j * 128:(j + 1) * 128], 0.0)
        square_buf[e, j:j + 1, :] = jnp.sum(picked, axis=0, keepdims=True)
    squares_out = mates(lambda m: square_buf.at[e], square_buf.at[e], 5, "expert", e, n_expert)

    for c in merge_req:
        c.wait_recv()
    out = merged_out[r].astype(jnp.float32)
    for s in range(1, n_req):
        out += merged_in[lax.rem(r + n_req - s, n_req)].astype(jnp.float32)
    verify_ref[...] = out.astype(jnp.bfloat16)

    relay(6)
    ring_step(2, scaled_buf, 1)
    relay(7)
    ring_step(2, scaled_buf, 2)
    relay(8)
    ring_step(2, scaled_buf, 3)
    for c in squares_out:
        c.wait_recv()
    total = square_buf[0]
    for b in range(1, n_expert):
        total += square_buf[b]
    spread = [
        jnp.sum(jnp.where(lane == line, total[j:j + 1], 0.0), axis=1, keepdims=True)
        for j in range(height // 128)
    ]
    width = block * n_expert
    scale = lax.rsqrt(jnp.concatenate(spread, axis=0) / width + EPS)

    sibfar = lax.rem(sib + half, n_req)
    piece_rows, wide = 256, gate_ref.shape[1]
    steps = gate_ref.shape[0] // (2 * piece_rows)
    homes = ((r, gate_ref, up_ref, down_ref), (sib, gate_sib, up_sib, down_sib),
             (partner, gate_far, up_far, down_far), (sibfar, gate_sibfar, up_sibfar, down_sibfar))

    def project_fetch(t):
        home, slot = homes[t // steps], t % 2
        copies = []
        for w, buf in ((home[1], gate_buf), (home[2], up_buf)):
            for q in range(2):
                rows_at = pl.ds((t % steps * 2 + q) * piece_rows, piece_rows)
                copies.append(pltpu.make_async_copy(
                    w.at[rows_at], buf.at[slot, pl.ds(0, piece_rows), pl.ds(q * 2048, wide)],
                    stream_sem.at[slot, len(copies)]))
        return copies

    def start(copies):
        for c in copies:
            c.start()

    def project(first, stop):
        start(project_fetch(first))
        for t in range(first, stop):
            if t + 1 < stop:
                start(project_fetch(t + 1))
            for c in project_fetch(t):
                c.wait()
            slot, index = t % 2, homes[t // steps][0]
            for buf, acc in ((gate_buf, gate_acc), (up_buf, up_acc)):
                def columns(at, buf=buf, acc=acc, slot=slot, index=index, t=t):
                    value = 0.0 if t == 0 else acc[:, at]
                    for q in range(2):
                        x = scaled_buf[index, :, pl.ds((t % steps * 2 + q) * piece_rows, piece_rows)]
                        w = buf[slot, pl.ds(0, piece_rows), pl.ds(pl.multiple_of(q * 2048 + at.start, 256), at.size)]
                        value += jnp.dot(x, w, preferred_element_type=jnp.float32)
                    acc[:, at] = value

                tiled(wide, 256, columns)

    for c in sib_out:
        c.wait_recv()
    project(0, 2 * steps)
    relay(9)
    for c in range(2 * cuts):
        to_sib(c, 2).wait_recv()
        to_sib(c, 3).wait_recv()
    project(2 * steps, 4 * steps)

    def activate(at):
        gate = gate_acc[:, at] * scale
        value = gate / (1.0 + jnp.exp(-gate)) * (up_acc[:, at] * scale)
        hidden_buf[:, at] = value.astype(jnp.bfloat16)

    tiled(wide, 256, activate)
    relay(10)

    pieces = down_ref.shape[0] // piece_rows
    ring_finish(0, near_all)

    def down_fetch(t):
        slot = t % 2
        return [
            pltpu.make_async_copy(
                homes[t][3].at[pl.ds(q * piece_rows, piece_rows)],
                (gate_buf, up_buf)[q // 4].at[slot, pl.ds(0, piece_rows), pl.ds(q % 4 * block, block)],
                stream_sem.at[slot, q])
            for q in range(pieces)
        ]

    def down(first, stop):
        start(down_fetch(first))
        for t in range(first, stop):
            if t + 1 < stop:
                start(down_fetch(t + 1))
            for c in down_fetch(t):
                c.wait()
            def columns(at, t=t):
                value = 0.0
                for q in range(pieces):
                    w = (gate_buf, up_buf)[q // 4][
                        t % 2, pl.ds(0, piece_rows), pl.ds(pl.multiple_of(q % 4 * block + at.start, 256), at.size)]
                    x = hidden_buf[:, pl.ds(q * piece_rows, piece_rows)]
                    value += jnp.dot(x, w, preferred_element_type=jnp.float32)
                near_all[homes[t][0], :, at] = value.astype(jnp.bfloat16)

            tiled(block, 256, columns)

    down(0, 2)
    relay(11)
    relay_last(count - 1)
    for c in range(2 * cuts, count):
        to_sib(c, 2).wait_recv()
        to_sib(c, 3).wait_recv()
    down(2, 4)

    def sum_left(p):
        return remote(near_all.at[p], sum_in.at[0, p], sum_send.at[0, p], sum_recv.at[0, p],
                      expert=lax.rem(e + n_expert - 1, n_expert))

    def sum_right(p):
        return remote(near_all.at[p], sum_in.at[1, p], sum_send.at[1, p], sum_recv.at[1, p],
                      expert=lax.rem(e + 1, n_expert))

    def add(p, way):
        both = near_all[p].astype(jnp.float32) + sum_in[way, p].astype(jnp.float32)
        near_all[p] = both.astype(jnp.bfloat16)

    for dist in range(n_expert - 1, 0, -1):
        @pl.when(e >= dist)
        def _():
            @pl.when(e < n_expert - 1)
            def _():
                sum_left(e - dist).wait_recv()
                add(e - dist, 0)

            sum_left(e - dist).start()

        @pl.when(e + dist < n_expert)
        def _():
            @pl.when(e > 0)
            def _():
                sum_right(e + dist).wait_recv()
                add(e + dist, 1)

            sum_right(e + dist).start()

    sent_acc[...] = near_acc[...] + near_all[e].astype(jnp.float32)

    @pl.when(e < n_expert - 1)
    def _():
        sum_left(e).wait_recv()
        sent_acc[...] += sum_in[0, e].astype(jnp.float32)

    @pl.when(e > 0)
    def _():
        sum_right(e).wait_recv()
        sent_acc[...] += sum_in[1, e].astype(jnp.float32)

    out_ref[...] = sent_acc[...].astype(jnp.bfloat16)
    for dist in range(1, n_expert):
        @pl.when(e >= dist)
        def _():
            sum_left(e - dist).wait_send()

        @pl.when(e + dist < n_expert)
        def _():
            sum_right(e + dist).wait_send()

    for c in rows_req + routes_out + rows_exp + merge_exp + merge_req + squares_out + sib_out:
        c.wait_send()
    for c in (cross, join_out, swap):
        c.wait_send()
    ring_finish(1, far_all)
    ring_finish(2, scaled_buf)
    for c in range(count):
        over_req(c).wait_send()
        over_group(c).wait_send()
        to_sib(c, 2).wait_send()
        to_sib(c, 3).wait_send()


def front(
    mine, theirs, gain, verify_in, routes, join_weight, draft_gate, draft_up, draft_down,
    moe_gate, moe_up, moe_down,
):
    n_expert, n_req, n_group = (lax.axis_size(a) for a in ("expert", "req", "group"))
    moe_gate, moe_up = moe_gate.transpose(0, 2, 1), moe_up.transpose(0, 2, 1)
    local, ff, width = moe_gate.shape
    slices = local * n_expert // EXPERTS
    rows, block = mine.shape
    own_rows, own_width = verify_in.shape
    bf, f32 = jnp.bfloat16, jnp.float32
    vmem, hbm = pl.BlockSpec(memory_space=pltpu.VMEM), pl.BlockSpec(memory_space=pl.ANY)
    weights = (draft_gate, draft_up, draft_down)
    like = [jax.ShapeDtypeStruct(w.shape, w.dtype) for w in weights]
    dma = pltpu.SemaphoreType.DMA
    n_chunks = 3 * CUTS
    big = max(n_expert, n_req)
    return pl.pallas_call(
        functools.partial(whole_kernel, (n_expert, n_req, n_group, slices)),
        out_shape=[
            jax.ShapeDtypeStruct(verify_in.shape, bf),
            jax.ShapeDtypeStruct((rows, block), bf),
            *like, *like, *like,
        ],
        in_specs=[vmem] * 5 + [hbm] * 7,
        out_specs=[vmem] * 2 + [hbm] * 9,
        scratch_shapes=[
            pltpu.VMEM((n_expert, rows, block), bf),
            pltpu.VMEM((n_expert, rows, block), bf),
            pltpu.VMEM((rows, block), f32),
            pltpu.VMEM((rows, block), f32),
            pltpu.VMEM((rows, block), bf),
            pltpu.VMEM((rows, block), bf),
            pltpu.VMEM((n_req // 2, *join_weight.shape), bf),
            pltpu.VMEM((n_expert, 8, 128), f32),
            pltpu.VMEM((n_expert, rows, block), bf),
            pltpu.VMEM((n_expert, own_rows, width), bf),
            pltpu.VMEM((n_expert, *routes.shape), f32),
            pltpu.VMEM((2, ff, width), bf),
            pltpu.VMEM((2, ff, width), bf),
            pltpu.VMEM((2, ff, width), bf),
            pltpu.VMEM((n_expert * own_rows, width), f32),
            pltpu.VMEM((n_expert, own_rows, width), bf),
            pltpu.VMEM((n_expert, own_rows, width), bf),
            pltpu.VMEM((n_req, own_rows, own_width), bf),
            pltpu.VMEM((n_req, own_rows, own_width), bf),
            dma((3, n_expert)), dma((3, n_expert)), dma((3, n_expert)),
            dma((6,)), dma((6,)), dma((2,)), dma((3, 2)),
            dma((6, big)), dma((6, big)), dma((4, n_chunks)), dma((4, n_chunks)),
            pltpu.VMEM((rows, draft_gate.shape[1]), f32),
            pltpu.VMEM((rows, draft_gate.shape[1]), f32),
            pltpu.VMEM((rows, draft_gate.shape[1]), bf),
            pltpu.VMEM((2, n_expert, rows, block), bf),
            dma((2, 8)), dma((2, n_expert)), dma((2, n_expert)),
        ],
        compiler_params=pltpu.CompilerParams(
            collective_id=0, has_side_effects=True, vmem_limit_bytes=58 * 2**20
        ),
        name="whole",
    )(mine, theirs, gain, verify_in, routes, join_weight, *weights, moe_gate, moe_up, moe_down)


def fused(
    verify_in, expert_ids, gate_weights, moe_gate, moe_up, moe_down,
    draft_emb, draft_feat, parents, join_weight, norm_gain, draft_gate, draft_up, draft_down,
):
    n_expert, n_req = lax.axis_size("expert"), lax.axis_size("req")
    r = lax.axis_index("req")
    side = r // (n_req // 2)
    rows = draft_emb.shape[0]
    feat = jnp.take(draft_feat, parents - r * rows, axis=0)
    mine = jnp.where(side == 0, draft_emb, feat)
    theirs = jnp.where(side == 0, feat, draft_emb)
    routes = jnp.concatenate([expert_ids.astype(jnp.float32), gate_weights], axis=1)
    routes = jnp.pad(routes, ((0, 0), (0, 128 - routes.shape[1])))
    verify_out, draft_out, *_ = front(
        mine, theirs, norm_gain[None, :], verify_in, routes, join_weight,
        draft_gate, draft_up, draft_down, moe_gate, moe_up, moe_down,
    )
    return verify_out, draft_out


def per_device(
    verify_in,
    expert_ids,
    gate_weights,
    moe_gate,
    moe_up,
    moe_down,
    draft_emb,
    draft_feat,
    parents,
    join_weight,
    norm_gain,
    draft_gate,
    draft_up,
    draft_down,
):
    n_expert, n_req = lax.axis_size("expert"), lax.axis_size("req")
    block, rows = draft_emb.shape[1], draft_emb.shape[0]
    fits = (
        n_req == 4 and lax.axis_size("group") == 2 and n_expert == 4
        and join_weight.shape[0] % block == 0 and draft_gate.shape[0] == block
        and block % 256 == 0 and draft_gate.shape[1] % 128 == 0
        and rows % 128 == 0 and rows <= 1024 and expert_ids.shape[1] == 2
        and draft_gate.shape[1] <= 2048 and draft_gate.shape[1] % 256 == 0 and draft_down.shape[1] == block == 1024
        and draft_gate.shape[0] % 512 == 0 and draft_down.shape[0] % 256 == 0
        and draft_down.shape[0] <= 2048 and moe_gate.shape[0] % 4 == 0
        and moe_gate.shape[1] == 4096 and moe_gate.shape[2] >= 256
    )
    if fits:
        return fused(
            verify_in, expert_ids, gate_weights, moe_gate, moe_up, moe_down,
            draft_emb, draft_feat, parents, join_weight, norm_gain,
            draft_gate, draft_up, draft_down,
        )
    draft_out = draft_step(
        draft_emb, draft_feat, parents, join_weight, norm_gain, draft_gate, draft_up, draft_down
    )
    verify_out = verify_layer(verify_in, expert_ids, gate_weights, moe_gate, moe_up, moe_down)
    return (verify_out, draft_out)


def solution(mesh):
    in_specs = (
        P(("group", "expert"), "req"),
        P(("group", "expert"), None),
        P(("group", "expert"), None),
        P("expert", None, "req"),
        P("expert", None, "req"),
        P("expert", "req", None),
        P(("group", "req"), "expert"),
        P(("group", "req"), "expert"),
        P(("group", "req")),
        P("req", "expert"),
        P("expert"),
        P("req", "expert"),
        P("req", "expert"),
        P("expert", "req"),
    )
    out_specs = (P(("group", "expert"), "req"), P(("group", "req"), "expert"))
    return jax.shard_map(
        per_device, mesh=mesh, in_specs=in_specs, out_specs=out_specs, check_vma=False
    )
```

```python
import functools

import jax
import jax.numpy as jnp
from jax import lax
from jax.experimental import pallas as pl
from jax.experimental.pallas import tpu as pltpu
from jax.sharding import PartitionSpec as P

EXPERTS = 8
EPS = 1e-05
CUTS = 4
AHEAD = 3


def verify_layer(verify_in, expert_ids, gate_weights, moe_gate, moe_up, moe_down):
    n_expert, n_req = lax.axis_size("expert"), lax.axis_size("req")
    own_rows, own_width = verify_in.shape
    local = moe_gate.shape[0]
    slices = local * n_expert // EXPERTS
    rows, width = own_rows * n_expert, own_width * n_req

    blocks = lax.all_gather(verify_in, ("expert", "req"), axis=0)
    blocks = blocks.reshape(n_expert, n_req, own_rows, own_width)
    hidden_in = blocks.transpose(0, 2, 1, 3).reshape(rows, width)
    routes = jnp.concatenate([expert_ids.astype(jnp.float32), gate_weights], axis=1)
    routes = lax.all_gather(routes, "expert", axis=0, tiled=True)
    top = expert_ids.shape[1]
    ids, gains = routes[:, :top].astype(jnp.int32), routes[:, top:]
    held = (lax.axis_index("expert") * local + jnp.arange(local, dtype=jnp.int32)) // slices
    mixing = jnp.sum(
        jnp.where(ids[None] == held[:, None, None], gains[None], 0.0), axis=2
    )

    batch = jnp.broadcast_to(hidden_in[None], (local, rows, width))
    gate = jnp.einsum("kmd,kdf->kmf", batch, moe_gate, preferred_element_type=jnp.float32)
    up = jnp.einsum("kmd,kdf->kmf", batch, moe_up, preferred_element_type=jnp.float32)
    hidden = (jax.nn.silu(gate) * up * mixing[:, :, None]).astype(jnp.bfloat16)
    hidden = hidden.transpose(1, 0, 2).reshape(rows, -1)
    down = moe_down.reshape(-1, width)
    partial = jnp.dot(hidden, down, preferred_element_type=jnp.float32).astype(jnp.bfloat16)
    partial = partial.reshape(n_expert, own_rows, n_req, own_width).transpose(0, 2, 1, 3)
    partial = partial.reshape(n_expert * n_req, own_rows, own_width)
    out = lax.psum_scatter(partial, ("expert", "req"), scatter_dimension=0)
    return out.astype(jnp.bfloat16)


def draft_step(
    draft_emb, draft_feat, parents, join_weight, norm_gain, draft_gate, draft_up, draft_down
):
    n_expert, n_req = lax.axis_size("expert"), lax.axis_size("req")
    n_group = lax.axis_size("group")
    r, g = lax.axis_index("req"), lax.axis_index("group")
    half = n_req // 2
    side, place = r // half, r % half
    rows, width = draft_emb.shape[0], draft_emb.shape[1] * n_expert

    def across(x):
        return lax.ppermute(x, "req", [(i, (i + half) % n_req) for i in range(n_req)])

    def within(x, step):
        return lax.ppermute(
            x,
            "req",
            [(i // half * half + (i + step) % half, i) for i in range(n_req)],
        )

    def other_group(x, step):
        return lax.ppermute(x, "group", [((i + step) % n_group, i) for i in range(n_group)])

    def pieces_of(weight):
        found = [(side * half + (place + s) % half, None, weight if s == 0 else within(weight, s))
                 for s in range(half)]
        depth = weight.shape[0] // n_group
        part = lax.dynamic_slice_in_dim(weight, g * depth, depth, axis=0)
        crossed = across(part)
        far = [(g, crossed)]
        far += [((g + s) % n_group, other_group(crossed, s)) for s in range(1, n_group)]
        for s in range(half):
            index = (1 - side) * half + (place + s) % half
            found += [(index, p, a if s == 0 else within(a, s)) for p, a in far]
        return found

    local_parent = parents - r * rows
    feat = jnp.take(draft_feat, local_parent, axis=0)
    mine = jnp.where(side == 0, draft_emb, feat)
    theirs = across(jnp.where(side == 0, feat, draft_emb))
    join_pieces = [
        ((place + s) % half, join_weight if s == 0 else within(join_weight, s))
        for s in range(half)
    ]
    depth = join_weight.shape[0]

    def join(block):
        whole = lax.all_gather(block, "expert", axis=1, tiled=True)
        return sum(
            jnp.dot(
                lax.dynamic_slice_in_dim(whole, index * depth, depth, axis=1),
                weight,
                preferred_element_type=jnp.float32,
            )
            for index, weight in join_pieces
        )

    kept = join(mine)
    sent = join(theirs)
    joined_state = kept + across(sent.astype(jnp.bfloat16)).astype(jnp.float32)

    squares = lax.psum(jnp.sum(joined_state * joined_state, axis=1), "expert")
    scale = lax.rsqrt(squares[:, None] / width + EPS)
    scaled = (joined_state * norm_gain[None, :]).astype(jnp.bfloat16)
    inputs = lax.all_gather(scaled, "expert", axis=1, tiled=True)

    def project(weight):
        total = 0.0
        full = weight.shape[0]
        for index, part, array in pieces_of(weight):
            start = index * full if part is None else index * full + part * array.shape[0]
            columns = lax.dynamic_slice_in_dim(inputs, start, array.shape[0], axis=1)
            total += jnp.dot(columns, array, preferred_element_type=jnp.float32)
        return total

    gate = project(draft_gate) * scale
    up = project(draft_up) * scale
    hidden = (jax.nn.silu(gate) * up).astype(jnp.bfloat16)

    near, far = [], []
    full = draft_down.shape[0]
    pieces = pieces_of(draft_down)
    for s in range(half):
        near.append(jnp.dot(hidden, pieces[s][2], preferred_element_type=jnp.float32))
    for s in range(half):
        total = 0.0
        for _, part, array in pieces[half + s * n_group : half + (s + 1) * n_group]:
            columns = lax.dynamic_slice_in_dim(hidden, part * array.shape[0], array.shape[0], axis=1)
            total += jnp.dot(columns, array, preferred_element_type=jnp.float32)
        far.append(total)

    def ordered(blocks):
        stack = jnp.stack(blocks).astype(jnp.bfloat16)
        order = (jnp.arange(half) - place) % half
        return stack[order]

    near, far = ordered(near), ordered(far)
    both = jnp.where(side == 0, jnp.concatenate([near, far]), jnp.concatenate([far, near]))
    terms = both.transpose(1, 0, 2).reshape(rows, width)
    mlp_sum = lax.psum_scatter(terms, "expert", scatter_dimension=1, tiled=True)
    return (joined_state + mlp_sum.astype(jnp.float32)).astype(jnp.bfloat16)


def whole_kernel(
    shape,
    mine_ref, theirs_ref, gain_ref, rows_ref, routes_ref,
    join_ref, gate_ref, up_ref, down_ref, moe_gate_ref, moe_up_ref, moe_down_ref,
    verify_ref, out_ref,
    gate_sib, up_sib, down_sib, gate_far, up_far, down_far, gate_sibfar, up_sibfar, down_sibfar,
    near_all, far_all, near_acc, sent_acc, swap_out, swap_in, join_all, square_buf, scaled_buf,
    row_all, route_all, gate_buf, up_buf, down_buf, moe_acc, moe_out, moe_in, merged_out, merged_in,
    ring_send_r, ring_send_l, ring_recv, misc_send, misc_recv, local_sem, moe_sem,
    mate_send, mate_recv, wide_send, wide_recv,
    gate_acc, up_acc, hidden_buf, sum_in, stream_sem, sum_send, sum_recv,
):
    n_expert, n_req, n_group, slices = shape
    half = n_req // 2
    g, e, r = lax.axis_index("group"), lax.axis_index("expert"), lax.axis_index("req")
    place = lax.rem(r, half)
    sib = r + 1 - 2 * place
    partner = lax.rem(r + half, n_req)

    def remote(src, dst, send, recv, **where):
        return pltpu.make_async_remote_copy(
            src_ref=src, dst_ref=dst, send_sem=send, recv_sem=recv,
            device_id=where, device_id_type=pl.DeviceIdType.MESH,
        )

    barrier = pltpu.get_barrier_semaphore()
    for s in range(1, n_req):
        pl.semaphore_signal(barrier, inc=1, device_id={"req": lax.rem(r + s, n_req)},
                            device_id_type=pl.DeviceIdType.MESH)
    for s in range(1, n_expert):
        pl.semaphore_signal(barrier, inc=1, device_id={"expert": lax.rem(e + s, n_expert)},
                            device_id_type=pl.DeviceIdType.MESH)
    pl.semaphore_signal(barrier, inc=1, device_id={"group": 1 - g},
                        device_id_type=pl.DeviceIdType.MESH)

    local = moe_gate_ref.shape[0]

    def fetch(k, slot):
        return [
            pltpu.make_async_copy(w.at[k], b.at[slot], moe_sem.at[i, slot])
            for i, (w, b) in enumerate(
                ((moe_gate_ref, gate_buf), (moe_up_ref, up_buf), (moe_down_ref, down_buf)))
        ]

    for c in fetch(0, 0):
        c.start()
    own_join = pltpu.make_async_copy(join_ref, join_all.at[place], local_sem.at[0])
    own_join.start()
    own_width = rows_ref.shape[1]
    own_columns = pl.ds(pl.multiple_of(r * own_width, own_width), own_width)
    near_all[e] = mine_ref[...]
    row_all[e, :, own_columns] = rows_ref[...]
    route_all[e] = routes_ref[...]
    pl.semaphore_wait(barrier, n_req + n_expert - 1)

    def to_right(i, buf, b):
        return remote(buf.at[b], buf.at[b], ring_send_r.at[i, b], ring_recv.at[i, b],
                      expert=lax.rem(e + 1, n_expert))

    def to_left(i, buf, b):
        return remote(buf.at[b], buf.at[b], ring_send_l.at[i, b], ring_recv.at[i, b],
                      expert=lax.rem(e + n_expert - 1, n_expert))

    def ring_start(i, buf):
        @pl.when(e < n_expert - 1)
        def _():
            to_right(i, buf, e).start()

        @pl.when(e > 0)
        def _():
            to_left(i, buf, e).start()

    def ring_step(i, buf, s):
        @pl.when(e >= s)
        def _():
            to_right(i, buf, e - s).wait_recv()

            @pl.when(e < n_expert - 1)
            def _():
                to_right(i, buf, e - s).start()

        @pl.when(e + s < n_expert)
        def _():
            to_left(i, buf, e + s).wait_recv()

            @pl.when(e > 0)
            def _():
                to_left(i, buf, e + s).start()

    def ring_finish(i, buf):
        for b in range(n_expert):
            @pl.when((b <= e) & (e < n_expert - 1))
            def _():
                to_right(i, buf, b).wait_send()

            @pl.when((b >= e) & (e > 0))
            def _():
                to_left(i, buf, b).wait_send()

    def mates(buf_of, dst_of, row, axis, me, n):
        copies = []
        for s in range(1, n):
            mate = lax.rem(me + s, n)
            c = remote(buf_of(mate), dst_of, mate_send.at[row, s], mate_recv.at[row, s], **{axis: mate})
            c.start()
            copies.append(c)
        return copies

    cross = remote(theirs_ref, far_all.at[e], misc_send.at[0], misc_recv.at[0], req=partner)
    cross.start()
    rows_req = mates(lambda m: rows_ref, row_all.at[e, :, own_columns], 0, "req", r, n_req)
    routes_out = mates(lambda m: routes_ref, route_all.at[e], 1, "expert", e, n_expert)
    ring_start(0, near_all)
    join_out = remote(join_ref, join_all.at[place], misc_send.at[1], misc_recv.at[1], req=sib)
    join_out.start()
    for c in rows_req:
        c.wait_recv()
    rows_exp = mates(lambda m: row_all.at[e], row_all.at[e], 2, "expert", e, n_expert)
    sib_out = []
    for i, (w, d) in enumerate(((gate_ref, gate_sib), (up_ref, up_sib), (down_ref, down_sib))):
        c = remote(w, d, misc_send.at[2 + i], misc_recv.at[2 + i], req=sib)
        c.start()
        sib_out.append(c)

    weights = ((gate_ref, gate_far, gate_sibfar), (up_ref, up_far, up_sibfar), (down_ref, down_far, down_sibfar))
    cuts = CUTS
    chunks = []
    for own, far, sibfar in weights:
        part = own.shape[0] // n_group
        piece = part // cuts
        for cut in range(cuts):
            chunks.append((own, far, sibfar, part, piece, cut * piece))

    def span(c, owner):
        _, _, _, part, piece, start = chunks[c]
        return pl.ds(pl.multiple_of(owner * part + start, 16), piece)

    def over_req(c):
        at = span(c, g)
        return remote(chunks[c][0].at[at], chunks[c][1].at[at], wide_send.at[0, c], wide_recv.at[0, c], req=partner)

    def over_group(c):
        at = span(c, g)
        return remote(chunks[c][1].at[at], chunks[c][1].at[at], wide_send.at[1, c], wide_recv.at[1, c], group=1 - g)

    def to_sib(c, which):
        at = span(c, g if which == 2 else 1 - g)
        return remote(chunks[c][1].at[at], chunks[c][2].at[at], wide_send.at[which, c], wide_recv.at[which, c], req=sib)

    count = len(chunks)

    def relay(c):
        over_req(c).wait_recv()
        if c + AHEAD < count:
            over_req(c + AHEAD).start()
        over_group(c).start()
        to_sib(c, 2).start()
        if c > 0:
            relay_last(c - 1)

    def relay_last(c):
        over_group(c).wait_recv()
        to_sib(c, 3).start()

    cross.wait_recv()
    ring_start(1, far_all)
    for c in range(AHEAD):
        over_req(c).start()
    for c in rows_exp + routes_out:
        c.wait_recv()
    moe_acc[...] = jnp.zeros_like(moe_acc)
    own_rows = rows_ref.shape[0]
    rows = own_rows * n_expert

    def tiled(width, size, body):
        def step(n, carry):
            body(pl.ds(pl.multiple_of(n * size, size), size))
            return carry

        lax.fori_loop(0, width // size, step, 0)

    def expert_piece(k, carry):
        slot = lax.rem(k, 2)

        @pl.when(k + 1 < local)
        def _():
            for c in fetch(k + 1, 1 - slot):
                c.start()

        for c in fetch(k, slot):
            c.wait()
        x = row_all[...].reshape(rows, row_all.shape[2])
        routes = route_all[...].reshape(rows, route_all.shape[2])
        expert = ((e * local + k) // slices).astype(jnp.float32)
        mixing = jnp.where(routes[:, 0:1] == expert, routes[:, 2:3], 0.0)
        mixing += jnp.where(routes[:, 1:2] == expert, routes[:, 3:4], 0.0)
        last = (((1,), (1,)), ((), ()))
        a = lax.dot_general(x, gate_buf[slot], last, preferred_element_type=jnp.float32)
        b = lax.dot_general(x, up_buf[slot], last, preferred_element_type=jnp.float32)
        hidden = (a / (1.0 + jnp.exp(-a)) * b * mixing).astype(jnp.bfloat16)

        def columns(at):
            moe_acc[:, at] += jnp.dot(hidden, down_buf[slot, :, at], preferred_element_type=jnp.float32)

        tiled(row_all.shape[2], 512, columns)
        return carry

    def moe(start, stop):
        lax.fori_loop(start, stop, expert_piece, 0)

    block = near_all.shape[2]
    per = join_ref.shape[0] // block
    tile = 256

    def join(buf, acc):
        def columns(at):
            total = 0.0
            for b in range(n_expert):
                w = join_all[b // per, pl.ds(b % per * block, block), at]
                total += jnp.dot(buf[b], w, preferred_element_type=jnp.float32)
            acc[:, at] = total

        tiled(acc.shape[1], tile, columns)

    quarter = local // 4
    moe(0, quarter)
    ring_step(1, far_all, 1)
    relay(0)
    moe(quarter, 2 * quarter)
    ring_step(1, far_all, 2)
    relay(1)
    moe(2 * quarter, 3 * quarter)
    ring_step(1, far_all, 3)
    ring_step(0, near_all, 1)
    own_join.wait()
    join_out.wait_recv()
    join(far_all, sent_acc)
    swap_out[...] = sent_acc[...].astype(jnp.bfloat16)
    swap = remote(swap_out, swap_in, misc_send.at[5], misc_recv.at[5], req=partner)
    swap.start()
    relay(2)
    moe(3 * quarter, local)
    ring_step(0, near_all, 2)
    relay(3)

    moe_out[...] = moe_acc[...].astype(jnp.bfloat16).reshape(moe_out.shape)
    merge_exp = mates(lambda m: moe_out.at[m], moe_in.at[e], 3, "expert", e, n_expert)
    ring_step(0, near_all, 3)
    join(near_all, near_acc)

    swap.wait_recv()
    height = near_acc.shape[0]
    sums = jnp.zeros((height, 1), jnp.float32)
    for n in range(block // tile):
        at = pl.ds(n * tile, tile)
        state = near_acc[:, at] + swap_in[:, at].astype(jnp.float32)
        near_acc[:, at] = state
        scaled_buf[e, :, at] = (state * gain_ref[:, at]).astype(jnp.bfloat16)
        sums += jnp.sum(state * state, axis=1, keepdims=True)
    ring_start(2, scaled_buf)
    lane = lax.broadcasted_iota(jnp.int32, (128, 128), 1)
    line = lax.broadcasted_iota(jnp.int32, (128, 128), 0)
    for j in range(height // 128):
        picked = jnp.where(lane == line, sums[j * 128:(j + 1) * 128], 0.0)
        square_buf[e, j:j + 1, :] = jnp.sum(picked, axis=0, keepdims=True)
    squares_out = mates(lambda m: square_buf.at[e], square_buf.at[e], 5, "expert", e, n_expert)

    relay(4)
    for c in merge_exp:
        c.wait_recv()
    merged = moe_out[e].astype(jnp.float32)
    for s in range(1, n_expert):
        merged += moe_in[lax.rem(e + n_expert - s, n_expert)].astype(jnp.float32)
    for j in range(n_req):
        merged_out[j] = merged[:, j * own_width:(j + 1) * own_width].astype(jnp.bfloat16)
    merge_req = mates(lambda m: merged_out.at[m], merged_in.at[r], 4, "req", r, n_req)

    relay(5)
    ring_step(2, scaled_buf, 1)
    relay(6)
    for c in merge_req:
        c.wait_recv()
    out = merged_out[r].astype(jnp.float32)
    for s in range(1, n_req):
        out += merged_in[lax.rem(r + n_req - s, n_req)].astype(jnp.float32)
    verify_ref[...] = out.astype(jnp.bfloat16)

    ring_step(2, scaled_buf, 2)
    relay(7)
    ring_step(2, scaled_buf, 3)
    relay(8)
    for c in squares_out:
        c.wait_recv()
    total = square_buf[0]
    for b in range(1, n_expert):
        total += square_buf[b]
    spread = [
        jnp.sum(jnp.where(lane == line, total[j:j + 1], 0.0), axis=1, keepdims=True)
        for j in range(height // 128)
    ]
    width = block * n_expert
    scale = lax.rsqrt(jnp.concatenate(spread, axis=0) / width + EPS)

    sibfar = lax.rem(sib + half, n_req)
    piece_rows, wide = 256, gate_ref.shape[1]
    steps = gate_ref.shape[0] // (2 * piece_rows)
    homes = ((r, gate_ref, up_ref, down_ref), (sib, gate_sib, up_sib, down_sib),
             (partner, gate_far, up_far, down_far), (sibfar, gate_sibfar, up_sibfar, down_sibfar))

    def project_fetch(t):
        home, slot = homes[t // steps], t % 2
        copies = []
        for w, buf in ((home[1], gate_buf), (home[2], up_buf)):
            for q in range(2):
                rows_at = pl.ds((t % steps * 2 + q) * piece_rows, piece_rows)
                copies.append(pltpu.make_async_copy(
                    w.at[rows_at], buf.at[slot, pl.ds(0, piece_rows), pl.ds(q * 2048, wide)],
                    stream_sem.at[slot, len(copies)]))
        return copies

    def start(copies):
        for c in copies:
            c.start()

    def project(first, stop):
        start(project_fetch(first))
        for t in range(first, stop):
            if t + 1 < stop:
                start(project_fetch(t + 1))
            for c in project_fetch(t):
                c.wait()
            slot, index = t % 2, homes[t // steps][0]
            for buf, acc in ((gate_buf, gate_acc), (up_buf, up_acc)):
                def columns(at, buf=buf, acc=acc, slot=slot, index=index, t=t):
                    value = 0.0 if t == 0 else acc[:, at]
                    for q in range(2):
                        x = scaled_buf[index, :, pl.ds((t % steps * 2 + q) * piece_rows, piece_rows)]
                        w = buf[slot, pl.ds(0, piece_rows), pl.ds(pl.multiple_of(q * 2048 + at.start, 256), at.size)]
                        value += jnp.dot(x, w, preferred_element_type=jnp.float32)
                    acc[:, at] = value

                tiled(wide, 256, columns)

    for c in sib_out:
        c.wait_recv()
    project(0, 2 * steps)
    for c in range(2 * cuts):
        to_sib(c, 2).wait_recv()
        to_sib(c, 3).wait_recv()
    project(2 * steps, 4 * steps)

    def activate(at):
        gate = gate_acc[:, at] * scale
        value = gate / (1.0 + jnp.exp(-gate)) * (up_acc[:, at] * scale)
        hidden_buf[:, at] = value.astype(jnp.bfloat16)

    tiled(wide, 256, activate)
    relay(9)

    pieces = down_ref.shape[0] // piece_rows
    ring_finish(0, near_all)

    def down_fetch(t):
        slot = t % 2
        return [
            pltpu.make_async_copy(
                homes[t][3].at[pl.ds(q * piece_rows, piece_rows)],
                (gate_buf, up_buf)[q // 4].at[slot, pl.ds(0, piece_rows), pl.ds(q % 4 * block, block)],
                stream_sem.at[slot, q])
            for q in range(pieces)
        ]

    def down(first, stop):
        start(down_fetch(first))
        for t in range(first, stop):
            if t + 1 < stop:
                start(down_fetch(t + 1))
            for c in down_fetch(t):
                c.wait()
            def columns(at, t=t):
                value = 0.0
                for q in range(pieces):
                    w = (gate_buf, up_buf)[q // 4][
                        t % 2, pl.ds(0, piece_rows), pl.ds(pl.multiple_of(q % 4 * block + at.start, 256), at.size)]
                    x = hidden_buf[:, pl.ds(q * piece_rows, piece_rows)]
                    value += jnp.dot(x, w, preferred_element_type=jnp.float32)
                near_all[homes[t][0], :, at] = value.astype(jnp.bfloat16)

            tiled(block, 256, columns)

    def sum_left(p):
        return remote(near_all.at[p], sum_in.at[0, p], sum_send.at[0, p], sum_recv.at[0, p],
                      expert=lax.rem(e + n_expert - 1, n_expert))

    def sum_right(p):
        return remote(near_all.at[p], sum_in.at[1, p], sum_send.at[1, p], sum_recv.at[1, p],
                      expert=lax.rem(e + 1, n_expert))

    def add(p, way):
        both = near_all[p].astype(jnp.float32) + sum_in[way, p].astype(jnp.float32)
        near_all[p] = both.astype(jnp.bfloat16)

    def pass_on(dist, of_side):
        @pl.when((e >= dist) & ((e - dist) // half == of_side))
        def _():
            @pl.when(e < n_expert - 1)
            def _():
                sum_left(e - dist).wait_recv()
                add(e - dist, 0)

            sum_left(e - dist).start()

        @pl.when((e + dist < n_expert) & ((e + dist) // half == of_side))
        def _():
            @pl.when(e > 0)
            def _():
                sum_right(e + dist).wait_recv()
                add(e + dist, 1)

            sum_right(e + dist).start()

    side = r // half
    down(0, 2)
    for dist in range(n_expert - 1, 0, -1):
        pass_on(dist, side)
        if dist == 2:
            relay(10)
    relay(11)
    relay_last(count - 1)
    for c in range(2 * cuts, count):
        to_sib(c, 2).wait_recv()
        to_sib(c, 3).wait_recv()
    down(2, 4)
    for dist in range(n_expert - 1, 0, -1):
        pass_on(dist, 1 - side)

    sent_acc[...] = near_acc[...] + near_all[e].astype(jnp.float32)

    @pl.when(e < n_expert - 1)
    def _():
        sum_left(e).wait_recv()
        sent_acc[...] += sum_in[0, e].astype(jnp.float32)

    @pl.when(e > 0)
    def _():
        sum_right(e).wait_recv()
        sent_acc[...] += sum_in[1, e].astype(jnp.float32)

    out_ref[...] = sent_acc[...].astype(jnp.bfloat16)
    for dist in range(1, n_expert):
        @pl.when(e >= dist)
        def _():
            sum_left(e - dist).wait_send()

        @pl.when(e + dist < n_expert)
        def _():
            sum_right(e + dist).wait_send()

    for c in rows_req + routes_out + rows_exp + merge_exp + merge_req + squares_out + sib_out:
        c.wait_send()
    for c in (cross, join_out, swap):
        c.wait_send()
    ring_finish(1, far_all)
    ring_finish(2, scaled_buf)
    for c in range(count):
        over_req(c).wait_send()
        over_group(c).wait_send()
        to_sib(c, 2).wait_send()
        to_sib(c, 3).wait_send()


def front(
    mine, theirs, gain, verify_in, routes, join_weight, draft_gate, draft_up, draft_down,
    moe_gate, moe_up, moe_down,
):
    n_expert, n_req, n_group = (lax.axis_size(a) for a in ("expert", "req", "group"))
    moe_gate, moe_up = moe_gate.transpose(0, 2, 1), moe_up.transpose(0, 2, 1)
    local, ff, width = moe_gate.shape
    slices = local * n_expert // EXPERTS
    rows, block = mine.shape
    own_rows, own_width = verify_in.shape
    bf, f32 = jnp.bfloat16, jnp.float32
    vmem, hbm = pl.BlockSpec(memory_space=pltpu.VMEM), pl.BlockSpec(memory_space=pl.ANY)
    weights = (draft_gate, draft_up, draft_down)
    like = [jax.ShapeDtypeStruct(w.shape, w.dtype) for w in weights]
    dma = pltpu.SemaphoreType.DMA
    n_chunks = 3 * CUTS
    big = max(n_expert, n_req)
    return pl.pallas_call(
        functools.partial(whole_kernel, (n_expert, n_req, n_group, slices)),
        out_shape=[
            jax.ShapeDtypeStruct(verify_in.shape, bf),
            jax.ShapeDtypeStruct((rows, block), bf),
            *like, *like, *like,
        ],
        in_specs=[vmem] * 5 + [hbm] * 7,
        out_specs=[vmem] * 2 + [hbm] * 9,
        scratch_shapes=[
            pltpu.VMEM((n_expert, rows, block), bf),
            pltpu.VMEM((n_expert, rows, block), bf),
            pltpu.VMEM((rows, block), f32),
            pltpu.VMEM((rows, block), f32),
            pltpu.VMEM((rows, block), bf),
            pltpu.VMEM((rows, block), bf),
            pltpu.VMEM((n_req // 2, *join_weight.shape), bf),
            pltpu.VMEM((n_expert, 8, 128), f32),
            pltpu.VMEM((n_expert, rows, block), bf),
            pltpu.VMEM((n_expert, own_rows, width), bf),
            pltpu.VMEM((n_expert, *routes.shape), f32),
            pltpu.VMEM((2, ff, width), bf),
            pltpu.VMEM((2, ff, width), bf),
            pltpu.VMEM((2, ff, width), bf),
            pltpu.VMEM((n_expert * own_rows, width), f32),
            pltpu.VMEM((n_expert, own_rows, width), bf),
            pltpu.VMEM((n_expert, own_rows, width), bf),
            pltpu.VMEM((n_req, own_rows, own_width), bf),
            pltpu.VMEM((n_req, own_rows, own_width), bf),
            dma((3, n_expert)), dma((3, n_expert)), dma((3, n_expert)),
            dma((6,)), dma((6,)), dma((2,)), dma((3, 2)),
            dma((6, big)), dma((6, big)), dma((4, n_chunks)), dma((4, n_chunks)),
            pltpu.VMEM((rows, draft_gate.shape[1]), f32),
            pltpu.VMEM((rows, draft_gate.shape[1]), f32),
            pltpu.VMEM((rows, draft_gate.shape[1]), bf),
            pltpu.VMEM((2, n_expert, rows, block), bf),
            dma((2, 8)), dma((2, n_expert)), dma((2, n_expert)),
        ],
        compiler_params=pltpu.CompilerParams(
            collective_id=0, has_side_effects=True, vmem_limit_bytes=58 * 2**20
        ),
        name="whole",
    )(mine, theirs, gain, verify_in, routes, join_weight, *weights, moe_gate, moe_up, moe_down)


def fused(
    verify_in, expert_ids, gate_weights, moe_gate, moe_up, moe_down,
    draft_emb, draft_feat, parents, join_weight, norm_gain, draft_gate, draft_up, draft_down,
):
    n_expert, n_req = lax.axis_size("expert"), lax.axis_size("req")
    r = lax.axis_index("req")
    side = r // (n_req // 2)
    rows = draft_emb.shape[0]
    feat = jnp.take(draft_feat, parents - r * rows, axis=0)
    mine = jnp.where(side == 0, draft_emb, feat)
    theirs = jnp.where(side == 0, feat, draft_emb)
    routes = jnp.concatenate([expert_ids.astype(jnp.float32), gate_weights], axis=1)
    routes = jnp.pad(routes, ((0, 0), (0, 128 - routes.shape[1])))
    verify_out, draft_out, *_ = front(
        mine, theirs, norm_gain[None, :], verify_in, routes, join_weight,
        draft_gate, draft_up, draft_down, moe_gate, moe_up, moe_down,
    )
    return verify_out, draft_out


def per_device(
    verify_in,
    expert_ids,
    gate_weights,
    moe_gate,
    moe_up,
    moe_down,
    draft_emb,
    draft_feat,
    parents,
    join_weight,
    norm_gain,
    draft_gate,
    draft_up,
    draft_down,
):
    n_expert, n_req = lax.axis_size("expert"), lax.axis_size("req")
    block, rows = draft_emb.shape[1], draft_emb.shape[0]
    fits = (
        n_req == 4 and lax.axis_size("group") == 2 and n_expert == 4
        and join_weight.shape[0] % block == 0 and draft_gate.shape[0] == block
        and block % 256 == 0 and draft_gate.shape[1] % 128 == 0
        and rows % 128 == 0 and rows <= 1024 and expert_ids.shape[1] == 2
        and draft_gate.shape[1] <= 2048 and draft_gate.shape[1] % 256 == 0 and draft_down.shape[1] == block == 1024
        and draft_gate.shape[0] % 512 == 0 and draft_down.shape[0] % 256 == 0
        and draft_down.shape[0] <= 2048 and moe_gate.shape[0] % 4 == 0
        and moe_gate.shape[1] == 4096 and moe_gate.shape[2] >= 256
    )
    if fits:
        return fused(
            verify_in, expert_ids, gate_weights, moe_gate, moe_up, moe_down,
            draft_emb, draft_feat, parents, join_weight, norm_gain,
            draft_gate, draft_up, draft_down,
        )
    draft_out = draft_step(
        draft_emb, draft_feat, parents, join_weight, norm_gain, draft_gate, draft_up, draft_down
    )
    verify_out = verify_layer(verify_in, expert_ids, gate_weights, moe_gate, moe_up, moe_down)
    return (verify_out, draft_out)


def solution(mesh):
    in_specs = (
        P(("group", "expert"), "req"),
        P(("group", "expert"), None),
        P(("group", "expert"), None),
        P("expert", None, "req"),
        P("expert", None, "req"),
        P("expert", "req", None),
        P(("group", "req"), "expert"),
        P(("group", "req"), "expert"),
        P(("group", "req")),
        P("req", "expert"),
        P("expert"),
        P("req", "expert"),
        P("req", "expert"),
        P("expert", "req"),
    )
    out_specs = (P(("group", "expert"), "req"), P(("group", "req"), "expert"))
    return jax.shard_map(
        per_device, mesh=mesh, in_specs=in_specs, out_specs=out_specs, check_vma=False
    )
```

```python
import functools

import jax
import jax.numpy as jnp
from jax import lax
from jax.experimental import pallas as pl
from jax.experimental.pallas import tpu as pltpu
from jax.sharding import PartitionSpec as P

EXPERTS = 8
EPS = 1e-05
CUTS = 4
AHEAD = 5


def verify_layer(verify_in, expert_ids, gate_weights, moe_gate, moe_up, moe_down):
    n_expert, n_req = lax.axis_size("expert"), lax.axis_size("req")
    own_rows, own_width = verify_in.shape
    local = moe_gate.shape[0]
    slices = local * n_expert // EXPERTS
    rows, width = own_rows * n_expert, own_width * n_req

    blocks = lax.all_gather(verify_in, ("expert", "req"), axis=0)
    blocks = blocks.reshape(n_expert, n_req, own_rows, own_width)
    hidden_in = blocks.transpose(0, 2, 1, 3).reshape(rows, width)
    routes = jnp.concatenate([expert_ids.astype(jnp.float32), gate_weights], axis=1)
    routes = lax.all_gather(routes, "expert", axis=0, tiled=True)
    top = expert_ids.shape[1]
    ids, gains = routes[:, :top].astype(jnp.int32), routes[:, top:]
    held = (lax.axis_index("expert") * local + jnp.arange(local, dtype=jnp.int32)) // slices
    mixing = jnp.sum(
        jnp.where(ids[None] == held[:, None, None], gains[None], 0.0), axis=2
    )

    batch = jnp.broadcast_to(hidden_in[None], (local, rows, width))
    gate = jnp.einsum("kmd,kdf->kmf", batch, moe_gate, preferred_element_type=jnp.float32)
    up = jnp.einsum("kmd,kdf->kmf", batch, moe_up, preferred_element_type=jnp.float32)
    hidden = (jax.nn.silu(gate) * up * mixing[:, :, None]).astype(jnp.bfloat16)
    hidden = hidden.transpose(1, 0, 2).reshape(rows, -1)
    down = moe_down.reshape(-1, width)
    partial = jnp.dot(hidden, down, preferred_element_type=jnp.float32).astype(jnp.bfloat16)
    partial = partial.reshape(n_expert, own_rows, n_req, own_width).transpose(0, 2, 1, 3)
    partial = partial.reshape(n_expert * n_req, own_rows, own_width)
    out = lax.psum_scatter(partial, ("expert", "req"), scatter_dimension=0)
    return out.astype(jnp.bfloat16)


def draft_step(
    draft_emb, draft_feat, parents, join_weight, norm_gain, draft_gate, draft_up, draft_down
):
    n_expert, n_req = lax.axis_size("expert"), lax.axis_size("req")
    n_group = lax.axis_size("group")
    r, g = lax.axis_index("req"), lax.axis_index("group")
    half = n_req // 2
    side, place = r // half, r % half
    rows, width = draft_emb.shape[0], draft_emb.shape[1] * n_expert

    def across(x):
        return lax.ppermute(x, "req", [(i, (i + half) % n_req) for i in range(n_req)])

    def within(x, step):
        return lax.ppermute(
            x,
            "req",
            [(i // half * half + (i + step) % half, i) for i in range(n_req)],
        )

    def other_group(x, step):
        return lax.ppermute(x, "group", [((i + step) % n_group, i) for i in range(n_group)])

    def pieces_of(weight):
        found = [(side * half + (place + s) % half, None, weight if s == 0 else within(weight, s))
                 for s in range(half)]
        depth = weight.shape[0] // n_group
        part = lax.dynamic_slice_in_dim(weight, g * depth, depth, axis=0)
        crossed = across(part)
        far = [(g, crossed)]
        far += [((g + s) % n_group, other_group(crossed, s)) for s in range(1, n_group)]
        for s in range(half):
            index = (1 - side) * half + (place + s) % half
            found += [(index, p, a if s == 0 else within(a, s)) for p, a in far]
        return found

    local_parent = parents - r * rows
    feat = jnp.take(draft_feat, local_parent, axis=0)
    mine = jnp.where(side == 0, draft_emb, feat)
    theirs = across(jnp.where(side == 0, feat, draft_emb))
    join_pieces = [
        ((place + s) % half, join_weight if s == 0 else within(join_weight, s))
        for s in range(half)
    ]
    depth = join_weight.shape[0]

    def join(block):
        whole = lax.all_gather(block, "expert", axis=1, tiled=True)
        return sum(
            jnp.dot(
                lax.dynamic_slice_in_dim(whole, index * depth, depth, axis=1),
                weight,
                preferred_element_type=jnp.float32,
            )
            for index, weight in join_pieces
        )

    kept = join(mine)
    sent = join(theirs)
    joined_state = kept + across(sent.astype(jnp.bfloat16)).astype(jnp.float32)

    squares = lax.psum(jnp.sum(joined_state * joined_state, axis=1), "expert")
    scale = lax.rsqrt(squares[:, None] / width + EPS)
    scaled = (joined_state * norm_gain[None, :]).astype(jnp.bfloat16)
    inputs = lax.all_gather(scaled, "expert", axis=1, tiled=True)

    def project(weight):
        total = 0.0
        full = weight.shape[0]
        for index, part, array in pieces_of(weight):
            start = index * full if part is None else index * full + part * array.shape[0]
            columns = lax.dynamic_slice_in_dim(inputs, start, array.shape[0], axis=1)
            total += jnp.dot(columns, array, preferred_element_type=jnp.float32)
        return total

    gate = project(draft_gate) * scale
    up = project(draft_up) * scale
    hidden = (jax.nn.silu(gate) * up).astype(jnp.bfloat16)

    near, far = [], []
    full = draft_down.shape[0]
    pieces = pieces_of(draft_down)
    for s in range(half):
        near.append(jnp.dot(hidden, pieces[s][2], preferred_element_type=jnp.float32))
    for s in range(half):
        total = 0.0
        for _, part, array in pieces[half + s * n_group : half + (s + 1) * n_group]:
            columns = lax.dynamic_slice_in_dim(hidden, part * array.shape[0], array.shape[0], axis=1)
            total += jnp.dot(columns, array, preferred_element_type=jnp.float32)
        far.append(total)

    def ordered(blocks):
        stack = jnp.stack(blocks).astype(jnp.bfloat16)
        order = (jnp.arange(half) - place) % half
        return stack[order]

    near, far = ordered(near), ordered(far)
    both = jnp.where(side == 0, jnp.concatenate([near, far]), jnp.concatenate([far, near]))
    terms = both.transpose(1, 0, 2).reshape(rows, width)
    mlp_sum = lax.psum_scatter(terms, "expert", scatter_dimension=1, tiled=True)
    return (joined_state + mlp_sum.astype(jnp.float32)).astype(jnp.bfloat16)


def whole_kernel(
    shape,
    mine_ref, theirs_ref, gain_ref, rows_ref, routes_ref,
    join_ref, gate_ref, up_ref, down_ref, moe_gate_ref, moe_up_ref, moe_down_ref,
    verify_ref, out_ref,
    gate_sib, up_sib, down_sib, gate_far, up_far, down_far, gate_sibfar, up_sibfar, down_sibfar,
    near_all, far_all, near_acc, sent_acc, swap_out, swap_in, join_all, square_buf, scaled_buf,
    row_all, route_all, gate_buf, up_buf, down_buf, moe_acc, moe_out, moe_in, merged_out, merged_in,
    ring_send_r, ring_send_l, ring_recv, misc_send, misc_recv, local_sem, moe_sem,
    mate_send, mate_recv, wide_send, wide_recv,
    gate_acc, up_acc, hidden_buf, sum_in, stream_sem, sum_send, sum_recv,
):
    n_expert, n_req, n_group, slices = shape
    half = n_req // 2
    g, e, r = lax.axis_index("group"), lax.axis_index("expert"), lax.axis_index("req")
    place = lax.rem(r, half)
    sib = r + 1 - 2 * place
    partner = lax.rem(r + half, n_req)

    def remote(src, dst, send, recv, **where):
        return pltpu.make_async_remote_copy(
            src_ref=src, dst_ref=dst, send_sem=send, recv_sem=recv,
            device_id=where, device_id_type=pl.DeviceIdType.MESH,
        )

    barrier = pltpu.get_barrier_semaphore()
    for s in range(1, n_req):
        pl.semaphore_signal(barrier, inc=1, device_id={"req": lax.rem(r + s, n_req)},
                            device_id_type=pl.DeviceIdType.MESH)
    for s in range(1, n_expert):
        pl.semaphore_signal(barrier, inc=1, device_id={"expert": lax.rem(e + s, n_expert)},
                            device_id_type=pl.DeviceIdType.MESH)
    pl.semaphore_signal(barrier, inc=1, device_id={"group": 1 - g},
                        device_id_type=pl.DeviceIdType.MESH)

    local = moe_gate_ref.shape[0]

    def fetch(k, slot):
        return [
            pltpu.make_async_copy(w.at[k], b.at[slot], moe_sem.at[i, slot])
            for i, (w, b) in enumerate(
                ((moe_gate_ref, gate_buf), (moe_up_ref, up_buf), (moe_down_ref, down_buf)))
        ]

    for c in fetch(0, 0):
        c.start()
    own_join = pltpu.make_async_copy(join_ref, join_all.at[place], local_sem.at[0])
    own_join.start()
    own_width = rows_ref.shape[1]
    own_columns = pl.ds(pl.multiple_of(r * own_width, own_width), own_width)
    near_all[e] = mine_ref[...]
    row_all[e, :, own_columns] = rows_ref[...]
    route_all[e] = routes_ref[...]
    pl.semaphore_wait(barrier, n_req + n_expert - 1)

    def to_right(i, buf, b):
        return remote(buf.at[b], buf.at[b], ring_send_r.at[i, b], ring_recv.at[i, b],
                      expert=lax.rem(e + 1, n_expert))

    def to_left(i, buf, b):
        return remote(buf.at[b], buf.at[b], ring_send_l.at[i, b], ring_recv.at[i, b],
                      expert=lax.rem(e + n_expert - 1, n_expert))

    def ring_start(i, buf):
        @pl.when(e < n_expert - 1)
        def _():
            to_right(i, buf, e).start()

        @pl.when(e > 0)
        def _():
            to_left(i, buf, e).start()

    def ring_step(i, buf, s):
        @pl.when(e >= s)
        def _():
            to_right(i, buf, e - s).wait_recv()

            @pl.when(e < n_expert - 1)
            def _():
                to_right(i, buf, e - s).start()

        @pl.when(e + s < n_expert)
        def _():
            to_left(i, buf, e + s).wait_recv()

            @pl.when(e > 0)
            def _():
                to_left(i, buf, e + s).start()

    def ring_finish(i, buf):
        for b in range(n_expert):
            @pl.when((b <= e) & (e < n_expert - 1))
            def _():
                to_right(i, buf, b).wait_send()

            @pl.when((b >= e) & (e > 0))
            def _():
                to_left(i, buf, b).wait_send()

    def mates(buf_of, dst_of, row, axis, me, n):
        copies = []
        for s in range(1, n):
            mate = lax.rem(me + s, n)
            c = remote(buf_of(mate), dst_of, mate_send.at[row, s], mate_recv.at[row, s], **{axis: mate})
            c.start()
            copies.append(c)
        return copies

    cross = remote(theirs_ref, far_all.at[e], misc_send.at[0], misc_recv.at[0], req=partner)
    cross.start()
    rows_req = mates(lambda m: rows_ref, row_all.at[e, :, own_columns], 0, "req", r, n_req)
    routes_out = mates(lambda m: routes_ref, route_all.at[e], 1, "expert", e, n_expert)
    ring_start(0, near_all)
    join_out = remote(join_ref, join_all.at[place], misc_send.at[1], misc_recv.at[1], req=sib)
    join_out.start()
    for c in rows_req:
        c.wait_recv()
    rows_exp = mates(lambda m: row_all.at[e], row_all.at[e], 2, "expert", e, n_expert)
    sib_out = []
    for i, (w, d) in enumerate(((gate_ref, gate_sib), (up_ref, up_sib), (down_ref, down_sib))):
        c = remote(w, d, misc_send.at[2 + i], misc_recv.at[2 + i], req=sib)
        c.start()
        sib_out.append(c)

    weights = ((gate_ref, gate_far, gate_sibfar), (up_ref, up_far, up_sibfar), (down_ref, down_far, down_sibfar))
    cuts = CUTS
    chunks = []
    for own, far, sibfar in weights:
        part = own.shape[0] // n_group
        piece = part // cuts
        for cut in range(cuts):
            chunks.append((own, far, sibfar, part, piece, cut * piece))

    def span(c, owner):
        _, _, _, part, piece, start = chunks[c]
        return pl.ds(pl.multiple_of(owner * part + start, 16), piece)

    def over_req(c):
        at = span(c, g)
        return remote(chunks[c][0].at[at], chunks[c][1].at[at], wide_send.at[0, c], wide_recv.at[0, c], req=partner)

    def over_group(c):
        at = span(c, g)
        return remote(chunks[c][1].at[at], chunks[c][1].at[at], wide_send.at[1, c], wide_recv.at[1, c], group=1 - g)

    def to_sib(c, which):
        at = span(c, g if which == 2 else 1 - g)
        return remote(chunks[c][1].at[at], chunks[c][2].at[at], wide_send.at[which, c], wide_recv.at[which, c], req=sib)

    count = len(chunks)

    def relay(c):
        over_req(c).wait_recv()
        if c + AHEAD < count:
            over_req(c + AHEAD).start()
        over_group(c).start()
        to_sib(c, 2).start()
        if c > 0:
            relay_last(c - 1)

    def relay_last(c):
        over_group(c).wait_recv()
        to_sib(c, 3).start()

    cross.wait_recv()
    ring_start(1, far_all)
    for c in range(AHEAD):
        over_req(c).start()
    for c in rows_exp + routes_out:
        c.wait_recv()
    moe_acc[...] = jnp.zeros_like(moe_acc)
    own_rows = rows_ref.shape[0]
    rows = own_rows * n_expert

    def tiled(width, size, body):
        def step(n, carry):
            body(pl.ds(pl.multiple_of(n * size, size), size))
            return carry

        lax.fori_loop(0, width // size, step, 0)

    def expert_piece(k, carry):
        slot = lax.rem(k, 2)

        @pl.when(k + 1 < local)
        def _():
            for c in fetch(k + 1, 1 - slot):
                c.start()

        for c in fetch(k, slot):
            c.wait()
        x = row_all[...].reshape(rows, row_all.shape[2])
        routes = route_all[...].reshape(rows, route_all.shape[2])
        expert = ((e * local + k) // slices).astype(jnp.float32)
        mixing = jnp.where(routes[:, 0:1] == expert, routes[:, 2:3], 0.0)
        mixing += jnp.where(routes[:, 1:2] == expert, routes[:, 3:4], 0.0)
        last = (((1,), (1,)), ((), ()))
        a = lax.dot_general(x, gate_buf[slot], last, preferred_element_type=jnp.float32)
        b = lax.dot_general(x, up_buf[slot], last, preferred_element_type=jnp.float32)
        hidden = (a / (1.0 + jnp.exp(-a)) * b * mixing).astype(jnp.bfloat16)

        def columns(at):
            moe_acc[:, at] += jnp.dot(hidden, down_buf[slot, :, at], preferred_element_type=jnp.float32)

        tiled(row_all.shape[2], 512, columns)
        return carry

    def moe(start, stop):
        lax.fori_loop(start, stop, expert_piece, 0)

    block = near_all.shape[2]
    per = join_ref.shape[0] // block
    tile = 256

    def join(buf, acc):
        def columns(at):
            total = 0.0
            for b in range(n_expert):
                w = join_all[b // per, pl.ds(b % per * block, block), at]
                total += jnp.dot(buf[b], w, preferred_element_type=jnp.float32)
            acc[:, at] = total

        tiled(acc.shape[1], tile, columns)

    quarter = local // 4
    moe(0, quarter)
    ring_step(1, far_all, 1)
    relay(0)
    moe(quarter, 2 * quarter)
    ring_step(1, far_all, 2)
    relay(1)
    moe(2 * quarter, 3 * quarter)
    ring_step(1, far_all, 3)
    ring_step(0, near_all, 1)
    own_join.wait()
    join_out.wait_recv()
    join(far_all, sent_acc)
    swap_out[...] = sent_acc[...].astype(jnp.bfloat16)
    swap = remote(swap_out, swap_in, misc_send.at[5], misc_recv.at[5], req=partner)
    swap.start()
    relay(2)
    moe(3 * quarter, local)
    ring_step(0, near_all, 2)
    relay(3)

    moe_out[...] = moe_acc[...].astype(jnp.bfloat16).reshape(moe_out.shape)
    merge_exp = mates(lambda m: moe_out.at[m], moe_in.at[e], 3, "expert", e, n_expert)
    ring_step(0, near_all, 3)
    join(near_all, near_acc)

    swap.wait_recv()
    height = near_acc.shape[0]
    sums = jnp.zeros((height, 1), jnp.float32)
    for n in range(block // tile):
        at = pl.ds(n * tile, tile)
        state = near_acc[:, at] + swap_in[:, at].astype(jnp.float32)
        near_acc[:, at] = state
        scaled_buf[e, :, at] = (state * gain_ref[:, at]).astype(jnp.bfloat16)
        sums += jnp.sum(state * state, axis=1, keepdims=True)
    ring_start(2, scaled_buf)
    lane = lax.broadcasted_iota(jnp.int32, (128, 128), 1)
    line = lax.broadcasted_iota(jnp.int32, (128, 128), 0)
    for j in range(height // 128):
        picked = jnp.where(lane == line, sums[j * 128:(j + 1) * 128], 0.0)
        square_buf[e, j:j + 1, :] = jnp.sum(picked, axis=0, keepdims=True)
    squares_out = mates(lambda m: square_buf.at[e], square_buf.at[e], 5, "expert", e, n_expert)

    relay(4)
    for c in merge_exp:
        c.wait_recv()
    merged = moe_out[e].astype(jnp.float32)
    for s in range(1, n_expert):
        merged += moe_in[lax.rem(e + n_expert - s, n_expert)].astype(jnp.float32)
    for j in range(n_req):
        merged_out[j] = merged[:, j * own_width:(j + 1) * own_width].astype(jnp.bfloat16)
    merge_req = mates(lambda m: merged_out.at[m], merged_in.at[r], 4, "req", r, n_req)

    relay(5)
    ring_step(2, scaled_buf, 1)
    relay(6)
    for c in merge_req:
        c.wait_recv()
    out = merged_out[r].astype(jnp.float32)
    for s in range(1, n_req):
        out += merged_in[lax.rem(r + n_req - s, n_req)].astype(jnp.float32)
    verify_ref[...] = out.astype(jnp.bfloat16)

    ring_step(2, scaled_buf, 2)
    relay(7)
    ring_step(2, scaled_buf, 3)
    relay(8)
    for c in squares_out:
        c.wait_recv()
    total = square_buf[0]
    for b in range(1, n_expert):
        total += square_buf[b]
    spread = [
        jnp.sum(jnp.where(lane == line, total[j:j + 1], 0.0), axis=1, keepdims=True)
        for j in range(height // 128)
    ]
    width = block * n_expert
    scale = lax.rsqrt(jnp.concatenate(spread, axis=0) / width + EPS)

    sibfar = lax.rem(sib + half, n_req)
    piece_rows, wide = 256, gate_ref.shape[1]
    steps = gate_ref.shape[0] // (2 * piece_rows)
    homes = ((r, gate_ref, up_ref, down_ref), (sib, gate_sib, up_sib, down_sib),
             (partner, gate_far, up_far, down_far), (sibfar, gate_sibfar, up_sibfar, down_sibfar))

    def project_fetch(t):
        home, slot = homes[t // steps], t % 2
        copies = []
        for w, buf in ((home[1], gate_buf), (home[2], up_buf)):
            for q in range(2):
                rows_at = pl.ds((t % steps * 2 + q) * piece_rows, piece_rows)
                copies.append(pltpu.make_async_copy(
                    w.at[rows_at], buf.at[slot, pl.ds(0, piece_rows), pl.ds(q * 2048, wide)],
                    stream_sem.at[slot, len(copies)]))
        return copies

    def start(copies):
        for c in copies:
            c.start()

    def project(first, stop):
        start(project_fetch(first))
        for t in range(first, stop):
            if t + 1 < stop:
                start(project_fetch(t + 1))
            for c in project_fetch(t):
                c.wait()
            slot, index = t % 2, homes[t // steps][0]
            for buf, acc in ((gate_buf, gate_acc), (up_buf, up_acc)):
                def columns(at, buf=buf, acc=acc, slot=slot, index=index, t=t):
                    value = 0.0 if t == 0 else acc[:, at]
                    for q in range(2):
                        x = scaled_buf[index, :, pl.ds((t % steps * 2 + q) * piece_rows, piece_rows)]
                        w = buf[slot, pl.ds(0, piece_rows), pl.ds(pl.multiple_of(q * 2048 + at.start, 256), at.size)]
                        value += jnp.dot(x, w, preferred_element_type=jnp.float32)
                    acc[:, at] = value

                tiled(wide, 256, columns)

    for c in sib_out:
        c.wait_recv()
    project(0, 2 * steps)
    for c in range(2 * cuts):
        to_sib(c, 2).wait_recv()
        to_sib(c, 3).wait_recv()
    project(2 * steps, 4 * steps)

    def activate(at):
        gate = gate_acc[:, at] * scale
        value = gate / (1.0 + jnp.exp(-gate)) * (up_acc[:, at] * scale)
        hidden_buf[:, at] = value.astype(jnp.bfloat16)

    tiled(wide, 256, activate)
    relay(9)

    pieces = down_ref.shape[0] // piece_rows
    ring_finish(0, near_all)

    def down_fetch(t):
        slot = t % 2
        return [
            pltpu.make_async_copy(
                homes[t][3].at[pl.ds(q * piece_rows, piece_rows)],
                (gate_buf, up_buf)[q // 4].at[slot, pl.ds(0, piece_rows), pl.ds(q % 4 * block, block)],
                stream_sem.at[slot, q])
            for q in range(pieces)
        ]

    def down(first, stop):
        start(down_fetch(first))
        for t in range(first, stop):
            if t + 1 < stop:
                start(down_fetch(t + 1))
            for c in down_fetch(t):
                c.wait()
            def columns(at, t=t):
                value = 0.0
                for q in range(pieces):
                    w = (gate_buf, up_buf)[q // 4][
                        t % 2, pl.ds(0, piece_rows), pl.ds(pl.multiple_of(q % 4 * block + at.start, 256), at.size)]
                    x = hidden_buf[:, pl.ds(q * piece_rows, piece_rows)]
                    value += jnp.dot(x, w, preferred_element_type=jnp.float32)
                near_all[homes[t][0], :, at] = value.astype(jnp.bfloat16)

            tiled(block, 256, columns)

    def sum_left(p):
        return remote(near_all.at[p], sum_in.at[0, p], sum_send.at[0, p], sum_recv.at[0, p],
                      expert=lax.rem(e + n_expert - 1, n_expert))

    def sum_right(p):
        return remote(near_all.at[p], sum_in.at[1, p], sum_send.at[1, p], sum_recv.at[1, p],
                      expert=lax.rem(e + 1, n_expert))

    def add(p, way):
        both = near_all[p].astype(jnp.float32) + sum_in[way, p].astype(jnp.float32)
        near_all[p] = both.astype(jnp.bfloat16)

    def pass_on(dist, of_side):
        @pl.when((e >= dist) & ((e - dist) // half == of_side))
        def _():
            @pl.when(e < n_expert - 1)
            def _():
                sum_left(e - dist).wait_recv()
                add(e - dist, 0)

            sum_left(e - dist).start()

        @pl.when((e + dist < n_expert) & ((e + dist) // half == of_side))
        def _():
            @pl.when(e > 0)
            def _():
                sum_right(e + dist).wait_recv()
                add(e + dist, 1)

            sum_right(e + dist).start()

    side = r // half
    down(0, 2)
    for dist in range(n_expert - 1, 0, -1):
        pass_on(dist, side)
        if dist == 2:
            relay(10)
    relay(11)
    relay_last(count - 1)
    for c in range(2 * cuts, count):
        to_sib(c, 2).wait_recv()
        to_sib(c, 3).wait_recv()
    down(2, 4)
    for dist in range(n_expert - 1, 0, -1):
        pass_on(dist, 1 - side)

    sent_acc[...] = near_acc[...] + near_all[e].astype(jnp.float32)

    @pl.when(e < n_expert - 1)
    def _():
        sum_left(e).wait_recv()
        sent_acc[...] += sum_in[0, e].astype(jnp.float32)

    @pl.when(e > 0)
    def _():
        sum_right(e).wait_recv()
        sent_acc[...] += sum_in[1, e].astype(jnp.float32)

    out_ref[...] = sent_acc[...].astype(jnp.bfloat16)
    for dist in range(1, n_expert):
        @pl.when(e >= dist)
        def _():
            sum_left(e - dist).wait_send()

        @pl.when(e + dist < n_expert)
        def _():
            sum_right(e + dist).wait_send()

    for c in rows_req + routes_out + rows_exp + merge_exp + merge_req + squares_out + sib_out:
        c.wait_send()
    for c in (cross, join_out, swap):
        c.wait_send()
    ring_finish(1, far_all)
    ring_finish(2, scaled_buf)
    for c in range(count):
        over_req(c).wait_send()
        over_group(c).wait_send()
        to_sib(c, 2).wait_send()
        to_sib(c, 3).wait_send()


def front(
    mine, theirs, gain, verify_in, routes, join_weight, draft_gate, draft_up, draft_down,
    moe_gate, moe_up, moe_down,
):
    n_expert, n_req, n_group = (lax.axis_size(a) for a in ("expert", "req", "group"))
    moe_gate, moe_up = moe_gate.transpose(0, 2, 1), moe_up.transpose(0, 2, 1)
    local, ff, width = moe_gate.shape
    slices = local * n_expert // EXPERTS
    rows, block = mine.shape
    own_rows, own_width = verify_in.shape
    bf, f32 = jnp.bfloat16, jnp.float32
    vmem, hbm = pl.BlockSpec(memory_space=pltpu.VMEM), pl.BlockSpec(memory_space=pl.ANY)
    weights = (draft_gate, draft_up, draft_down)
    like = [jax.ShapeDtypeStruct(w.shape, w.dtype) for w in weights]
    dma = pltpu.SemaphoreType.DMA
    n_chunks = 3 * CUTS
    big = max(n_expert, n_req)
    return pl.pallas_call(
        functools.partial(whole_kernel, (n_expert, n_req, n_group, slices)),
        out_shape=[
            jax.ShapeDtypeStruct(verify_in.shape, bf),
            jax.ShapeDtypeStruct((rows, block), bf),
            *like, *like, *like,
        ],
        in_specs=[vmem] * 5 + [hbm] * 7,
        out_specs=[vmem] * 2 + [hbm] * 9,
        scratch_shapes=[
            pltpu.VMEM((n_expert, rows, block), bf),
            pltpu.VMEM((n_expert, rows, block), bf),
            pltpu.VMEM((rows, block), f32),
            pltpu.VMEM((rows, block), f32),
            pltpu.VMEM((rows, block), bf),
            pltpu.VMEM((rows, block), bf),
            pltpu.VMEM((n_req // 2, *join_weight.shape), bf),
            pltpu.VMEM((n_expert, 8, 128), f32),
            pltpu.VMEM((n_expert, rows, block), bf),
            pltpu.VMEM((n_expert, own_rows, width), bf),
            pltpu.VMEM((n_expert, *routes.shape), f32),
            pltpu.VMEM((2, ff, width), bf),
            pltpu.VMEM((2, ff, width), bf),
            pltpu.VMEM((2, ff, width), bf),
            pltpu.VMEM((n_expert * own_rows, width), f32),
            pltpu.VMEM((n_expert, own_rows, width), bf),
            pltpu.VMEM((n_expert, own_rows, width), bf),
            pltpu.VMEM((n_req, own_rows, own_width), bf),
            pltpu.VMEM((n_req, own_rows, own_width), bf),
            dma((3, n_expert)), dma((3, n_expert)), dma((3, n_expert)),
            dma((6,)), dma((6,)), dma((2,)), dma((3, 2)),
            dma((6, big)), dma((6, big)), dma((4, n_chunks)), dma((4, n_chunks)),
            pltpu.VMEM((rows, draft_gate.shape[1]), f32),
            pltpu.VMEM((rows, draft_gate.shape[1]), f32),
            pltpu.VMEM((rows, draft_gate.shape[1]), bf),
            pltpu.VMEM((2, n_expert, rows, block), bf),
            dma((2, 8)), dma((2, n_expert)), dma((2, n_expert)),
        ],
        compiler_params=pltpu.CompilerParams(
            collective_id=0, has_side_effects=True, vmem_limit_bytes=58 * 2**20
        ),
        name="whole",
    )(mine, theirs, gain, verify_in, routes, join_weight, *weights, moe_gate, moe_up, moe_down)


def fused(
    verify_in, expert_ids, gate_weights, moe_gate, moe_up, moe_down,
    draft_emb, draft_feat, parents, join_weight, norm_gain, draft_gate, draft_up, draft_down,
):
    n_expert, n_req = lax.axis_size("expert"), lax.axis_size("req")
    r = lax.axis_index("req")
    side = r // (n_req // 2)
    rows = draft_emb.shape[0]
    feat = jnp.take(draft_feat, parents - r * rows, axis=0)
    mine = jnp.where(side == 0, draft_emb, feat)
    theirs = jnp.where(side == 0, feat, draft_emb)
    routes = jnp.concatenate([expert_ids.astype(jnp.float32), gate_weights], axis=1)
    routes = jnp.pad(routes, ((0, 0), (0, 128 - routes.shape[1])))
    verify_out, draft_out, *_ = front(
        mine, theirs, norm_gain[None, :], verify_in, routes, join_weight,
        draft_gate, draft_up, draft_down, moe_gate, moe_up, moe_down,
    )
    return verify_out, draft_out


def per_device(
    verify_in,
    expert_ids,
    gate_weights,
    moe_gate,
    moe_up,
    moe_down,
    draft_emb,
    draft_feat,
    parents,
    join_weight,
    norm_gain,
    draft_gate,
    draft_up,
    draft_down,
):
    n_expert, n_req = lax.axis_size("expert"), lax.axis_size("req")
    block, rows = draft_emb.shape[1], draft_emb.shape[0]
    fits = (
        n_req == 4 and lax.axis_size("group") == 2 and n_expert == 4
        and join_weight.shape[0] % block == 0 and draft_gate.shape[0] == block
        and block % 256 == 0 and draft_gate.shape[1] % 128 == 0
        and rows % 128 == 0 and rows <= 1024 and expert_ids.shape[1] == 2
        and draft_gate.shape[1] <= 2048 and draft_gate.shape[1] % 256 == 0 and draft_down.shape[1] == block == 1024
        and draft_gate.shape[0] % 512 == 0 and draft_down.shape[0] % 256 == 0
        and draft_down.shape[0] <= 2048 and moe_gate.shape[0] % 4 == 0
        and moe_gate.shape[1] == 4096 and moe_gate.shape[2] >= 256
    )
    if fits:
        return fused(
            verify_in, expert_ids, gate_weights, moe_gate, moe_up, moe_down,
            draft_emb, draft_feat, parents, join_weight, norm_gain,
            draft_gate, draft_up, draft_down,
        )
    draft_out = draft_step(
        draft_emb, draft_feat, parents, join_weight, norm_gain, draft_gate, draft_up, draft_down
    )
    verify_out = verify_layer(verify_in, expert_ids, gate_weights, moe_gate, moe_up, moe_down)
    return (verify_out, draft_out)


def solution(mesh):
    in_specs = (
        P(("group", "expert"), "req"),
        P(("group", "expert"), None),
        P(("group", "expert"), None),
        P("expert", None, "req"),
        P("expert", None, "req"),
        P("expert", "req", None),
        P(("group", "req"), "expert"),
        P(("group", "req"), "expert"),
        P(("group", "req")),
        P("req", "expert"),
        P("expert"),
        P("req", "expert"),
        P("req", "expert"),
        P("expert", "req"),
    )
    out_specs = (P(("group", "expert"), "req"), P(("group", "req"), "expert"))
    return jax.shard_map(
        per_device, mesh=mesh, in_specs=in_specs, out_specs=out_specs, check_vma=False
    )
```
